32 devices in a mesh: groups: 2 (over x), role: 2 (over core), seq: 8 (over z, y).
Axes of the slice: x: 2, y: 2, z: 4, core: 2. Of those that a mesh axis runs over, the one named last changes fastest.
Arguments:
- token_kv: bfloat16 [2, 8192, 2, 1024], P('role', ('groups', 'seq')), parts along dimension 1, may hold values from -6 to 6
- positions: int32 [2, 8192], P('role', ('groups', 'seq')), parts along dimension 1, may hold values from 0 to 131071, as said below
- page_owner: int32 [512], P(('groups', 'seq')), parts along dimension 0, may hold values from 0 to 7, as said below
- queries: bfloat16 [256, 8192], P('groups'), parts along dimension 0, may hold values from -220 to 220
- own_kv: bfloat16 [256, 2, 1024], P('groups'), parts along dimension 0, may hold values from -6 to 6
- selected: int32 [256, 8, 32], P('groups'), parts along dimension 0, may hold values from 0 to 1279, as said below
- lengths: int32 [256], P('groups'), parts along dimension 0, may hold values from 32768 to 131072
Outputs:
- attended: bfloat16 [256, 8192], P(('groups', 'role', 'seq')), parts along dimension 0
- bounds: float32 [256, 2048], P(('groups', 'role', 'seq')), parts along dimension 0
The draws below stay inside these ranges and needn't reach their ends.
There are 2 independent parts, one for each index of `groups`. The reference program is written for one: setup_inputs(seed, part) draws one part's arguments, and reference() takes and returns one part's arrays. A program takes and returns all parts, laid end to end along the dimension named above; each array names one. Nothing has to cross between parts.
Inputs may be any that keep to these rules, and one draw needn't show every extreme that they name: `page_owner`: among the 32 pages of one prefill device no owner appears more than 16 times, and one owner takes exactly 16 pages of every prefill device. `selected`: the 32 numbers of one row and key head are distinct numbers of existing pages. Within the 512 tokens of one device positions rise by one from a multiple of 16.
All inputs are finite; a program needn't handle non-finite values.
Results may differ from the reference program's by a relative error of at most 0.0075.
Values may be sent and summed in bfloat16 or wider, within the bound.
A program may use at most 128 MiB of HBM per device.

```python
import math
import jax
import jax.numpy as jnp
from jax import lax

QH = 64
KVH = 8
HD = 128
PAGE = 16
CTX = 131072
NSEL = 32
PT_DEV = 512
PAGE_DEV = 32
SLOT = 16
POOL_DEV = 160
NPAGE = 256
PTOK = 4096
ROWS = 128
N_SEQ = 8


def owner_table(key):
    key = jax.random.fold_in(key, 11)
    hot_owner = jax.random.randint(jax.random.fold_in(key, 1), (), 0, N_SEQ)
    shift_value = jax.random.randint(jax.random.fold_in(key, 2), (), 0, N_SEQ - 1)
    offsets = ((jnp.arange(N_SEQ, dtype=jnp.int32) + shift_value) % (N_SEQ - 1))[:, None]
    page_index = jnp.arange(PAGE_DEV)[None, :]
    spread = (offsets + (page_index - SLOT) // SLOT) % (N_SEQ - 1)
    owners = jnp.where(page_index < SLOT, hot_owner, (hot_owner + 1 + spread) % N_SEQ)

    def shuffle_block(block_key):
        return jax.random.permutation(block_key, PAGE_DEV)
    shuffles = jax.vmap(shuffle_block)(jax.random.split(jax.random.fold_in(key, 3), N_SEQ))
    owners = jnp.take_along_axis(owners, shuffles, axis=1)
    return owners.reshape(NPAGE).astype(jnp.int32)


def pool_numbers_drawn(owners):
    blocks = owners.reshape(N_SEQ, PAGE_DEV)
    same_owner = blocks[:, :, None] == blocks[:, None, :]
    earlier = jnp.arange(PAGE_DEV)[None, :] < jnp.arange(PAGE_DEV)[:, None]
    order_rank = jnp.sum(same_owner & earlier[None], axis=2).astype(jnp.int32)
    source = jnp.arange(N_SEQ, dtype=jnp.int32)[:, None]
    return (blocks * POOL_DEV + source * SLOT + order_rank).reshape(NPAGE).astype(jnp.int32)


def resident_numbers_drawn():
    page_index = jnp.arange(NPAGE, dtype=jnp.int32)
    return (page_index // PAGE_DEV * POOL_DEV + N_SEQ * SLOT + page_index % PAGE_DEV).astype(jnp.int32)


def draw_page_owner(key, part):
    return owner_table(key)


def draw_selected(key, part):
    live_numbers = jnp.concatenate([pool_numbers_drawn(owner_table(key)), resident_numbers_drawn()])
    key = jax.random.fold_in(key, 12)
    scores = jax.random.randint(key, (ROWS, KVH, 2 * NPAGE), 0, 2 ** 16) * (2 * NPAGE) + jnp.arange(2 * NPAGE, dtype=jnp.int32)
    picks = lax.top_k(scores, NSEL)[1]
    return live_numbers[picks].astype(jnp.int32)


def draw_positions(key, part):
    key = jax.random.fold_in(key, 13)
    start_page = jax.random.randint(key, (2 * N_SEQ, 1), 0, (CTX - PT_DEV) // PAGE + 1) * PAGE
    start_page = start_page.at[0, 0].set(0).at[1, 0].set(CTX - PT_DEV)
    drawn = start_page + jnp.arange(PT_DEV, dtype=jnp.int32)[None, :]
    return drawn.reshape(2, PTOK).astype(jnp.int32)


def draw_queries(key, part):
    key = jax.random.fold_in(key, 14)
    drawn = jnp.clip(jax.random.normal(key, (ROWS, QH * HD)), -6.0, 6.0)
    return drawn.astype(jnp.float32).astype(jnp.bfloat16)


def touch_ends(entries, key, low, high):
    shape = entries.shape
    place = [jax.random.randint(jax.random.fold_in(key, axis), (), 0, shape[axis]) for axis in range(len(shape))]
    entries = entries.at[tuple(place)].set(low)
    longest = shape.index(max(shape))
    place[longest] = (place[longest] + 1) % shape[longest]
    return entries.at[tuple(place)].set(high)


def levels(key, extent, cuts, low, top_value):
    def one(dim, blocks):
        heights = jax.random.uniform(jax.random.fold_in(jax.random.fold_in(key, 6), dim), (blocks,), jnp.float32, low / len(cuts), top_value / len(cuts))
        return jnp.repeat(jnp.exp(heights), extent[dim] // blocks).reshape((-1,) + (1,) * (len(extent) - dim - 1))

    loudness = one(*cuts[0])
    for cut in cuts[1:]:
        loudness = loudness * one(*cut)
    return loudness


def gaussian(key, shape, deviation, most, pieces=(), held_as=jnp.bfloat16):
    values = deviation * jax.random.normal(key, shape, jnp.float32)
    if pieces:
        values = values * levels(key, shape, pieces, -0.22, 0.18)
    return jnp.clip(values, -most, most).astype(held_as)


def setup_inputs(seed: int = 0, part: int = 0) -> dict:
    splits = jax.random.split(jax.random.key(seed), 8)
    part_keys = jax.random.split(jax.random.fold_in(splits[7], part), 8)
    return {
        "token_kv": gaussian(part_keys[0], (2, PTOK, 2, KVH * HD), 1.0, 6.0, ((0, 2), (1, 8))),
        "positions": draw_positions(jax.random.fold_in(jax.random.fold_in(splits[7], part), 71), part),
        "page_owner": draw_page_owner(jax.random.fold_in(jax.random.fold_in(splits[7], part), 71), part),
        "queries": draw_queries(jax.random.fold_in(jax.random.fold_in(splits[7], part), 71), part),
        "own_kv": gaussian(part_keys[4], (ROWS, 2, KVH * HD), 1.0, 6.0),
        "selected": draw_selected(jax.random.fold_in(jax.random.fold_in(splits[7], part), 71), part),
        "lengths": touch_ends(jax.random.randint(part_keys[6], (ROWS,), CTX // 4, CTX + 1), jax.random.fold_in(part_keys[6], 1), CTX // 4, CTX).astype(jnp.int32),
    }


NEG = -1e+30

def pool_numbers(owners):
    blocks = owners.reshape(N_SEQ, PAGE_DEV)
    same_owner = blocks[:, :, None] == blocks[:, None, :]
    earlier = jnp.arange(PAGE_DEV)[None, :] < jnp.arange(PAGE_DEV)[:, None]
    order_rank = lax.optimization_barrier(jnp.sum(same_owner & earlier[None], axis=2)).astype(jnp.int32)
    source = jnp.arange(N_SEQ, dtype=jnp.int32)[:, None]
    return (blocks * POOL_DEV + source * SLOT + order_rank).reshape(NPAGE).astype(jnp.int32)

def resident_numbers():
    page_index = jnp.arange(NPAGE, dtype=jnp.int32)
    return (page_index // PAGE_DEV * POOL_DEV + N_SEQ * SLOT + page_index % PAGE_DEV).astype(jnp.int32)

def reference(token_kv, positions, page_owner, queries, own_kv, selected, lengths):
    group_size = QH // KVH
    score_scale = 1.0 / math.sqrt(HD)
    page_blocks = token_kv.reshape(2 * NPAGE, PAGE, 2, KVH, HD)
    page_pos = positions.reshape(2 * NPAGE, PAGE)
    lookup = jnp.zeros((N_SEQ * POOL_DEV,), jnp.int32)
    lookup = lookup.at[pool_numbers(page_owner)].set(jnp.arange(NPAGE, dtype=jnp.int32))
    lookup = lookup.at[resident_numbers()].set(NPAGE + jnp.arange(NPAGE, dtype=jnp.int32))
    picked = lookup[selected]
    split_q = queries.reshape(ROWS, KVH, group_size, HD)
    split_own = own_kv.reshape(ROWS, 2, KVH, HD)

    def one_head(head_index):
        head_pages = lax.dynamic_index_in_dim(page_blocks, head_index, 3, keepdims=False)
        chosen = lax.dynamic_index_in_dim(picked, head_index, 1, keepdims=False)
        query_head = lax.dynamic_index_in_dim(split_q, head_index, 1, keepdims=False).astype(jnp.float32)
        key_rows = head_pages[chosen, :, 0, :].astype(jnp.float32)
        value_rows = head_pages[chosen, :, 1, :].astype(jnp.float32)
        usable = page_pos[chosen] < lengths[:, None, None]
        scores = jnp.einsum('rgd,rstd->rgst', query_head, key_rows) * score_scale
        masked = jnp.where(usable[:, None], scores, NEG)
        largest = lax.optimization_barrier(jnp.max(masked, axis=(2, 3)))
        weights = jnp.where(usable[:, None], jnp.exp(masked - largest[:, :, None, None]), 0.0)
        totals = lax.optimization_barrier(jnp.sum(weights, axis=(2, 3)))
        rounded = lax.optimization_barrier(weights.astype(jnp.bfloat16)).astype(jnp.float32)
        sums = jnp.einsum('rgst,rstd->rgd', rounded, value_rows)
        own_key = lax.dynamic_index_in_dim(split_own[:, 0], head_index, 1, keepdims=False).astype(jnp.float32)
        own_value = lax.dynamic_index_in_dim(split_own[:, 1], head_index, 1, keepdims=False).astype(jnp.float32)
        own_score = jnp.einsum('rgd,rd->rg', query_head, own_key) * score_scale
        highest = jnp.maximum(largest, own_score)
        fading = jnp.exp(largest - highest)
        fresh_weight = jnp.exp(own_score - highest)
        result = (sums * fading[..., None] + fresh_weight[..., None] * own_value[:, None, :]) / (totals * fading + fresh_weight)[..., None]
        top_key = lax.optimization_barrier(jnp.max(key_rows, axis=2))
        low_key = lax.optimization_barrier(jnp.min(key_rows, axis=2))
        spread_q = query_head[:, :, None, :]
        upper_bound = lax.optimization_barrier(jnp.sum(jnp.maximum(spread_q * top_key[:, None], spread_q * low_key[:, None]), axis=3)) * score_scale
        return (result, upper_bound)
    results, upper_bounds = lax.map(one_head, jnp.arange(KVH, dtype=jnp.int32))
    attended = jnp.transpose(results, (1, 0, 2, 3)).reshape(ROWS, QH * HD).astype(jnp.bfloat16)
    bounds = jnp.transpose(upper_bounds, (1, 0, 2, 3)).reshape(ROWS, QH * NSEL)
    return (attended, bounds)
```

```python
import functools
import math

import jax
import jax.numpy as jnp
from jax import lax
from jax.experimental import pallas as pl
from jax.experimental.pallas import tpu as pltpu
from jax.sharding import PartitionSpec as P

NEG = -1e30
LOG2E = 1.4426950408889634
MESH = pl.DeviceIdType.MESH


def from_behind(block, axis, distance):
    devices = range(lax.axis_size(axis))
    route = [(i - distance, i) for i in devices if i - distance in devices]
    return lax.ppermute(block, axis, route)


def owner_rank(owners):
    page_total = owners.shape[0]
    same_owner = owners[:, None] == owners[None, :]
    earlier = jnp.arange(page_total)[None, :] < jnp.arange(page_total)[:, None]
    return jnp.sum(same_owner & earlier, axis=1)


def pack_pages(target, slot_total, flat_kv, flat_sum, page_pos):
    chosen = jnp.arange(slot_total, dtype=jnp.int32)[:, None] == target[None, :]
    onehot = chosen.astype(jnp.bfloat16)
    sent_kv = jnp.dot(onehot, flat_kv, preferred_element_type=jnp.float32).astype(jnp.bfloat16)
    sent_sum = jnp.dot(onehot, flat_sum, preferred_element_type=jnp.float32).astype(jnp.bfloat16)
    sent_pos = jnp.sum(jnp.where(chosen[:, :, None], page_pos[None], 0), axis=1)
    return (sent_kv, sent_sum, sent_pos)


def attend(pool_kv, pool_sum, pool_pos, pool_ids, queries, selected, lengths, kv_heads):
    pool_total, page_len = pool_pos.shape
    kv_width = pool_kv.shape[-1]
    head_dim = kv_width // kv_heads
    row_total = queries.shape[0]
    group_size = queries.shape[1] // kv_width
    score_scale = 1.0 / math.sqrt(head_dim)
    token_total = pool_total * page_len
    row_block = 32
    block_count = row_total // row_block
    key_heads = jnp.transpose(
        pool_kv[:, :, 0, :].reshape(token_total, kv_heads, head_dim), (1, 0, 2)
    )
    value_heads = jnp.transpose(
        pool_kv[:, :, 1, :].reshape(token_total, kv_heads, head_dim), (1, 0, 2)
    )
    summary_heads = jnp.transpose(pool_sum.reshape(pool_total, 2, kv_heads, head_dim), (2, 0, 1, 3))
    timely = (pool_pos[None] < lengths[:, None, None]).reshape(
        block_count, row_block, pool_total, page_len
    )
    query_heads = jnp.transpose(
        queries.reshape(row_total, kv_heads, group_size, head_dim), (1, 0, 2, 3)
    )
    chosen_heads = jnp.transpose(selected, (1, 0, 2))

    def one_head(inputs):
        key_rows, value_rows, summary, query_head, chosen = inputs
        query_blocks = query_head.reshape(block_count, row_block, group_size, head_dim)
        chosen_blocks = chosen.reshape(block_count, row_block, chosen.shape[-1])

        def one_block(parts):
            query_block, chosen_block, timely_block = parts
            matches = chosen_block[:, :, None] == pool_ids[None, None, :]
            picked = jnp.any(matches, axis=1)
            usable = (picked[:, :, None] & timely_block).reshape(row_block, token_total)
            scores = (
                jnp.einsum("rgd,td->rgt", query_block, key_rows, preferred_element_type=jnp.float32)
                * score_scale
            )
            masked = jnp.where(usable[:, None, :], scores, NEG)
            largest = jnp.max(masked, axis=2)
            weights = jnp.where(usable[:, None, :], jnp.exp(masked - largest[:, :, None]), 0.0)
            totals = jnp.sum(weights, axis=2)
            sums = jnp.einsum(
                "rgt,td->rgd",
                weights.astype(jnp.bfloat16),
                value_rows,
                preferred_element_type=jnp.float32,
            )
            upper_part = jnp.maximum(query_block, 0)
            lower_part = jnp.maximum(-query_block, 0)
            upper_bound = jnp.einsum(
                "rgd,qd->rgq", upper_part, summary[:, 0], preferred_element_type=jnp.float32
            )
            upper_bound = (
                upper_bound
                - jnp.einsum(
                    "rgd,qd->rgq", lower_part, summary[:, 1], preferred_element_type=jnp.float32
                )
            ) * score_scale
            bound = jnp.einsum(
                "mfp,mlp->mlf",
                matches.astype(jnp.float32),
                upper_bound,
                precision=lax.Precision.HIGHEST,
            )
            return (largest, totals, sums, bound)

        largest, totals, sums, bound = lax.map(one_block, (query_blocks, chosen_blocks, timely))
        return (
            largest.reshape(row_total, group_size),
            totals.reshape(row_total, group_size),
            sums.reshape(row_total, group_size, head_dim),
            bound.reshape(row_total, group_size, -1),
        )

    largest, totals, sums, bounds = lax.map(
        one_head, (key_heads, value_heads, summary_heads, query_heads, chosen_heads)
    )
    largest = jnp.transpose(largest, (1, 0, 2)).reshape(row_total, kv_heads * group_size)
    totals = jnp.transpose(totals, (1, 0, 2)).reshape(row_total, kv_heads * group_size)
    sums = jnp.transpose(sums, (1, 0, 2, 3)).reshape(row_total, kv_heads * group_size, head_dim)
    bounds = jnp.transpose(bounds, (1, 0, 2, 3)).reshape(row_total, kv_heads * group_size, -1)
    return (largest, totals, sums, bounds)


def body(token_kv, positions, page_owner, queries, own_kv, selected, lengths):
    seq_total = lax.axis_size("seq")
    role_index = lax.axis_index("role")
    seq_index = lax.axis_index("seq")
    decoding = role_index == 1
    page_dev = page_owner.shape[0]
    tokens_dev = token_kv.shape[1]
    kv_width = token_kv.shape[3]
    page_len = tokens_dev // page_dev
    kv_heads = selected.shape[1]
    slot_count = max(2, 4 * page_dev // seq_total)
    inbound = seq_total * slot_count
    pool_dev = inbound + page_dev
    local_kv = token_kv[0].reshape(page_dev, page_len, 2, kv_width)
    local_pos = positions[0].reshape(page_dev, page_len)
    local_keys = local_kv[:, :, 0, :]
    local_sum = jnp.stack([jnp.max(local_keys, axis=1), jnp.min(local_keys, axis=1)], axis=1)
    order_rank = owner_rank(page_owner)
    flat_kv = local_kv.reshape(page_dev, page_len * 2 * kv_width)
    flat_sum = local_sum.reshape(page_dev, 2 * kv_width)
    out_kv, out_sum, out_pos = pack_pages(
        page_owner * slot_count + order_rank, inbound, flat_kv, flat_sum, local_pos
    )
    routed_kv, routed_sum, routed_pos = (
        lax.all_to_all(out_kv, "seq", split_axis=0, concat_axis=0, tiled=True),
        lax.all_to_all(out_sum, "seq", split_axis=0, concat_axis=0, tiled=True),
        lax.all_to_all(out_pos, "seq", split_axis=0, concat_axis=0, tiled=True),
    )
    got_kv, got_sum, got_pos = from_behind((routed_kv, routed_sum, routed_pos), "role", 1)
    pool_kv = jnp.concatenate([got_kv.reshape(inbound, page_len, 2, kv_width), local_kv], axis=0)
    pool_sum = jnp.concatenate([got_sum.reshape(inbound, 2, kv_width), local_sum], axis=0)
    pool_pos = jnp.concatenate([got_pos, local_pos], axis=0)
    pool_ids = jnp.where(decoding, seq_index * pool_dev + jnp.arange(pool_dev, dtype=jnp.int32), -1)
    largest, totals, sums, bounds = attend(
        pool_kv, pool_sum, pool_pos, pool_ids, queries, selected, lengths, kv_heads
    )
    row_total = queries.shape[0]
    device_total = 2 * seq_total
    rows_here = row_total // device_total
    first_row = (role_index * seq_total + seq_index) * rows_here
    overall = lax.pmax(largest, ("role", "seq"))
    factor = jnp.exp(largest - overall)
    sums, totals, bounds = (
        lax.psum_scatter(
            sums * factor[..., None], ("role", "seq"), scatter_dimension=0, tiled=True
        ),
        lax.psum_scatter(totals * factor, ("role", "seq"), scatter_dimension=0, tiled=True),
        lax.psum_scatter(bounds, ("role", "seq"), scatter_dimension=0, tiled=True),
    )
    largest = lax.dynamic_slice_in_dim(overall, first_row, rows_here, 0)
    head_dim = kv_width // kv_heads
    group_size = queries.shape[1] // kv_width
    score_scale = 1.0 / math.sqrt(head_dim)
    my_queries = lax.dynamic_slice_in_dim(queries, first_row, rows_here, 0).reshape(
        rows_here, kv_heads, group_size, head_dim
    )
    my_own = lax.dynamic_slice_in_dim(own_kv, first_row, rows_here, 0)
    own_keys = my_own[:, 0].reshape(rows_here, kv_heads, head_dim)
    own_values = my_own[:, 1].reshape(rows_here, kv_heads, 1, head_dim).astype(jnp.float32)
    own_score = (
        jnp.einsum(
            "rhgd,rhd->rhg", my_queries, own_keys, preferred_element_type=jnp.float32
        ).reshape(rows_here, kv_heads * group_size)
        * score_scale
    )
    highest = jnp.maximum(largest, own_score)
    fading = jnp.exp(largest - highest)
    fresh_weight = jnp.exp(own_score - highest)
    value_share = jnp.broadcast_to(own_values, (rows_here, kv_heads, group_size, head_dim)).reshape(
        rows_here, kv_heads * group_size, head_dim
    )
    attended = (sums * fading[..., None] + fresh_weight[..., None] * value_share) / (
        totals * fading + fresh_weight
    )[..., None]
    return (attended.reshape(rows_here, -1).astype(jnp.bfloat16), bounds.reshape(rows_here, -1))


def exchange_kernel(
    n_seq,
    heads,
    group,
    scale,
    ids_ref,
    lens_ref,
    pos_ref,
    sel_ref,
    own_ref,
    ownv_ref,
    q_hbm,
    kv_hbm,
    att_ref,
    bnd_ref,
    q_buf,
    kv_own,
    kv_got,
    pos_got,
    vt_buf,
    s_buf,
    p_buf,
    bias_buf,
    u_buf,
    mt_buf,
    lt_buf,
    send_buf,
    recv_buf,
    ml_send,
    ml_recv,
    load_sem,
    kv_send,
    kv_recv,
    o_send,
    o_recv,
):
    role = lax.axis_index("role")
    seq = lax.axis_index("seq")
    n_dev = 2 * n_seq
    me = role * n_seq + seq
    mate = {"role": 1 - role, "seq": seq}
    toks = kv_own.shape[1]
    hd = kv_own.shape[2] // 2
    pages = toks // 16
    rows = q_buf.shape[0]
    here = rows // n_dev
    half = q_buf.shape[1]

    q_copy = pltpu.make_async_copy(
        q_hbm.at[:, pl.ds(pl.multiple_of(role * half, half), half)], q_buf, load_sem.at[0]
    )
    q_copy.start()
    own_copy = pltpu.make_async_copy(kv_hbm.at[role], kv_own, load_sem.at[1])
    own_copy.start()

    barrier = pltpu.get_barrier_semaphore()

    def greet(j, carry):
        t = lax.rem(me + j, n_dev)
        pl.semaphore_signal(
            barrier, inc=1, device_id={"role": t // n_seq, "seq": t % n_seq}, device_id_type=MESH
        )
        return carry

    lax.fori_loop(1, n_dev, greet, 0)
    pl.semaphore_wait(barrier, n_dev - 1)

    def mate_copy(hl):
        return pltpu.make_async_remote_copy(
            src_ref=kv_hbm.at[1 - role, hl],
            dst_ref=kv_got.at[hl],
            send_sem=kv_send.at[hl],
            recv_sem=kv_recv.at[hl],
            device_id=mate,
            device_id_type=MESH,
        )

    pos_copy = pltpu.make_async_remote_copy(
        src_ref=pos_ref,
        dst_ref=pos_got,
        send_sem=kv_send.at[heads],
        recv_sem=kv_recv.at[heads],
        device_id=mate,
        device_id_type=MESH,
    )
    pos_copy.start()
    for hl in range(heads):
        mate_copy(hl).start()
    q_copy.wait()
    own_copy.wait()
    pos_copy.wait()

    mt_buf[...] = jnp.zeros_like(mt_buf)
    lt_buf[...] = jnp.zeros_like(lt_buf)

    def out_copy(hl, j):
        t = lax.rem(me + j, n_dev)
        return pltpu.make_async_remote_copy(
            src_ref=send_buf.at[hl, t],
            dst_ref=recv_buf.at[hl, me],
            send_sem=o_send.at[hl, t],
            recv_sem=o_recv.at[hl, me],
            device_id={"role": t // n_seq, "seq": t % n_seq},
            device_id_type=MESH,
        )

    def in_copy(hl, j):
        t = lax.rem(me + j, n_dev)
        return pltpu.make_async_remote_copy(
            src_ref=send_buf.at[hl, t],
            dst_ref=recv_buf.at[hl, t],
            send_sem=o_send.at[hl, t],
            recv_sem=o_recv.at[hl, t],
            device_id={"role": t // n_seq, "seq": t % n_seq},
            device_id_type=MESH,
        )

    def ml_out(j):
        t = lax.rem(me + j, n_dev)
        return pltpu.make_async_remote_copy(
            src_ref=ml_send.at[t],
            dst_ref=ml_recv.at[me],
            send_sem=o_send.at[heads, t],
            recv_sem=o_recv.at[heads, me],
            device_id={"role": t // n_seq, "seq": t % n_seq},
            device_id_type=MESH,
        )

    def ml_in(j):
        t = lax.rem(me + j, n_dev)
        return pltpu.make_async_remote_copy(
            src_ref=ml_send.at[t],
            dst_ref=ml_recv.at[t],
            send_sem=o_send.at[heads, t],
            recv_sem=o_recv.at[heads, t],
            device_id={"role": t // n_seq, "seq": t % n_seq},
            device_id_type=MESH,
        )

    lens = lens_ref[...]
    n_sel = sel_ref.shape[1]
    dims = (((1,), (1,)), ((), ()))

    def one_head(hl, carry):
        mate_copy(hl).wait()
        sel = sel_ref[role * heads + hl]
        ids = ids_ref[...]
        hit = jnp.zeros((2 * pages, rows), jnp.float32) + NEG
        for s in range(n_sel):
            hit = jnp.where(ids == sel[s : s + 1, :], 0.0, hit)
        for part in range(2):
            start = (pos_ref if part == 0 else pos_got)[0:1, :]
            left = lens - start
            wide = jnp.broadcast_to(
                hit[part * pages : (part + 1) * pages][:, None, :], (pages, 16, rows)
            ).reshape(toks, rows)
            place = lax.broadcasted_iota(jnp.int32, (toks, rows), 0)
            bias_buf[part * toks : (part + 1) * toks, :] = jnp.where(place < left, wide, NEG)

        tops = []
        lows = []
        for part in range(2):
            block = kv_own if part == 0 else kv_got
            k32 = block[hl, :, 0:hd].astype(jnp.float32).reshape(pages, 16, hd)
            tops.append(jnp.max(k32, axis=1))
            lows.append(jnp.min(k32, axis=1))
            v32 = block[hl, :, hd : 2 * hd].astype(jnp.float32)
            vt_buf[:, part * toks : (part + 1) * toks] = v32.T.astype(jnp.bfloat16)
        summary = jnp.concatenate(
            [jnp.concatenate(tops, axis=0), jnp.concatenate(lows, axis=0)], axis=1
        ).astype(jnp.bfloat16)

        def one_pair(gp, carry):
            outs = []
            for sub in range(2):
                g = gp * 2 + sub
                q = q_buf[:, pl.ds(pl.multiple_of((hl * group + g) * hd, hd), hd)]
                q32 = q.astype(jnp.float32)
                signed = jnp.concatenate(
                    [jnp.maximum(q32, 0.0), jnp.minimum(q32, 0.0)], axis=1
                ).astype(jnp.bfloat16)
                u_buf[g] = (
                    lax.dot_general(summary, signed, dims, preferred_element_type=jnp.float32)
                    * scale
                )
                for part in range(2):
                    block = kv_own if part == 0 else kv_got
                    s_buf[sub, part * toks : (part + 1) * toks, :] = (
                        lax.dot_general(
                            block[hl, :, 0:hd], q, dims, preferred_element_type=jnp.float32
                        )
                        * (scale * LOG2E)
                        + bias_buf[part * toks : (part + 1) * toks, :]
                    )
                top = jnp.max(s_buf[sub], axis=0, keepdims=True)
                w = jnp.exp2(s_buf[sub] - top)
                total = jnp.sum(w, axis=0, keepdims=True)
                p_buf[sub] = w.astype(jnp.bfloat16)
                o = jnp.dot(vt_buf[...], p_buf[sub], preferred_element_type=jnp.float32)
                o = o * (1.0 / total)
                mt_buf[pl.ds(hl * group + g, 1), :] = top
                lt_buf[pl.ds(hl * group + g, 1), :] = total
                outs.append(o.T.reshape(n_dev, here, hd))
            send_buf[hl, :, pl.ds(pl.multiple_of(gp * 2 * here, 2 * here), 2 * here), :] = (
                jnp.concatenate(outs, axis=1).astype(jnp.bfloat16)
            )
            return carry

        lax.fori_loop(0, group // 2, one_pair, 0)

        acc = [jnp.zeros((n_sel, rows), jnp.float32) for _ in range(group)]
        for p in range(2 * pages):
            same = sel == ids_ref[p : p + 1, :]
            for g in range(group):
                acc[g] = jnp.where(same, u_buf[g, p : p + 1, :], acc[g])
        gs = group // 2
        lefth = jnp.concatenate(acc[:gs], axis=0).T.reshape(n_dev, here, gs * n_sel)
        righth = jnp.concatenate(acc[gs:], axis=0).T.reshape(n_dev, here, gs * n_sel)
        send_buf[hl, :, group * here : group * here + 2 * here, :] = jnp.concatenate(
            [lefth, righth], axis=1
        ).astype(jnp.bfloat16)

        def go(j, carry):
            out_copy(hl, j).start()
            return carry

        lax.fori_loop(1, n_dev, go, 0)
        recv_buf[hl, me] = send_buf[hl, me]
        return carry

    lax.fori_loop(0, heads, one_head, 0)

    ml_send[:, 0:here, :] = mt_buf[...].T.reshape(n_dev, here, hd)
    ml_send[:, here : 2 * here, :] = lt_buf[...].T.reshape(n_dev, here, hd)

    def go_ml(j, carry):
        ml_out(j).start()
        return carry

    lax.fori_loop(1, n_dev, go_ml, 0)
    ml_recv[me] = ml_send[me]

    def end_ml(j, carry):
        ml_in(j).wait()
        return carry

    lax.fori_loop(1, n_dev, end_ml, 0)

    shares = []
    for r in range(2):
        mine = own_ref[r]
        tops = [ml_recv[r * n_seq + c, 0:here, :] for c in range(n_seq)]
        highest = mine
        for m in tops:
            highest = jnp.maximum(highest, m)
        fresh = jnp.exp2(mine - highest)
        parts = [
            jnp.exp2(tops[c] - highest) * ml_recv[r * n_seq + c, here : 2 * here, :]
            for c in range(n_seq)
        ]
        inv = fresh
        for w in parts:
            inv = inv + w
        inv = 1.0 / inv
        shares.append([w * inv for w in parts] + [fresh * inv])

    for hl in range(heads):

        def end(j, carry):
            in_copy(hl, j).wait()
            return carry

        lax.fori_loop(1, n_dev, end, 0)
        for r in range(2):
            h = r * heads + hl
            own_v = ownv_ref[:, h * hd : (h + 1) * hd]
            own_v = jnp.concatenate([own_v, own_v], axis=0)
            for gp in range(group // 2):
                j = hl * group + gp * 2

                def column(w):
                    return jnp.concatenate([w[:, j : j + 1], w[:, j + 1 : j + 2]], axis=0)

                total = column(shares[r][n_seq]) * own_v
                for c in range(n_seq):
                    block = recv_buf[
                        hl, r * n_seq + c, gp * 2 * here : (gp + 1) * 2 * here, :
                    ].astype(jnp.float32)
                    total = total + column(shares[r][c]) * block
                at = (h * group + gp * 2) * hd
                att_ref[:, at : at + hd] = total[0:here].astype(jnp.bfloat16)
                att_ref[:, at + hd : at + 2 * hd] = total[here : 2 * here].astype(jnp.bfloat16)
            bound = jnp.zeros((2 * here, hd), jnp.float32)
            for c in range(n_seq):
                bound = bound + recv_buf[
                    hl, r * n_seq + c, group * here : (group + 2) * here, :
                ].astype(jnp.float32)
            at = h * group * n_sel
            bnd_ref[:, at : at + hd] = bound[0:here]
            bnd_ref[:, at + hd : at + 2 * hd] = bound[here : 2 * here]


def direct_body(token_kv, positions, page_owner, queries, own_kv, selected, lengths):
    seq_total = lax.axis_size("seq")
    role_index = lax.axis_index("role")
    seq_index = lax.axis_index("seq")
    page_dev = page_owner.shape[0]
    toks = token_kv.shape[1]
    kv_width = token_kv.shape[3]
    rows, kv_heads, n_sel = selected.shape
    hd = kv_width // kv_heads
    group = queries.shape[1] // kv_width
    heads = kv_heads // 2
    scale = 1.0 / math.sqrt(hd)
    slot_count = max(2, 4 * page_dev // seq_total)
    inbound = seq_total * slot_count
    pool_dev = inbound + page_dev
    n_dev = 2 * seq_total
    here = rows // n_dev
    me = role_index * seq_total + seq_index

    new_ids = page_owner * pool_dev + seq_index * slot_count + owner_rank(page_owner)
    old_ids = seq_index * pool_dev + inbound + jnp.arange(page_dev, dtype=jnp.int32)
    ids = jnp.where(
        role_index == 0,
        jnp.concatenate([new_ids, old_ids]),
        jnp.concatenate([old_ids, new_ids]),
    )
    ids = jnp.broadcast_to(ids[:, None], (2 * page_dev, rows)).astype(jnp.int32)
    pos = jnp.broadcast_to(positions[:, 0:1], (8, rows))
    sel = jnp.transpose(selected, (1, 2, 0))
    kv = jnp.transpose(token_kv[0].reshape(toks, 2, 2, heads, hd), (2, 3, 0, 1, 4)).reshape(
        2, heads, toks, 2 * hd
    )
    my_q = lax.dynamic_slice_in_dim(queries, me * here, here, 0).reshape(
        here, kv_heads, group, hd
    )
    my_own = lax.dynamic_slice_in_dim(own_kv, me * here, here, 0)
    own_score = jnp.sum(
        my_q.astype(jnp.float32)
        * my_own[:, 0].reshape(here, kv_heads, 1, hd).astype(jnp.float32),
        axis=3,
    ) * (scale * LOG2E)
    own = jnp.transpose(own_score.reshape(here, 2, heads * group), (1, 0, 2))
    own = jnp.pad(own, ((0, 0), (0, 0), (0, 128 - heads * group)))
    own_v = my_own[:, 1].astype(jnp.float32)

    vmem = pl.BlockSpec(memory_space=pltpu.VMEM)
    hbm = pl.BlockSpec(memory_space=pl.ANY)
    block = (group + 2) * here
    return pl.pallas_call(
        functools.partial(exchange_kernel, seq_total, heads, group, scale),
        out_shape=(
            jax.ShapeDtypeStruct((here, kv_heads * group * hd), jnp.bfloat16),
            jax.ShapeDtypeStruct((here, kv_heads * group * n_sel), jnp.float32),
        ),
        in_specs=[vmem] * 6 + [hbm] * 2,
        out_specs=(vmem, vmem),
        scratch_shapes=[
            pltpu.VMEM((rows, heads * group * hd), jnp.bfloat16),
            pltpu.VMEM((heads, toks, 2 * hd), jnp.bfloat16),
            pltpu.VMEM((heads, toks, 2 * hd), jnp.bfloat16),
            pltpu.VMEM((8, rows), jnp.int32),
            pltpu.VMEM((hd, 2 * toks), jnp.bfloat16),
            pltpu.VMEM((2, 2 * toks, rows), jnp.float32),
            pltpu.VMEM((2, 2 * toks, rows), jnp.bfloat16),
            pltpu.VMEM((2 * toks, rows), jnp.float32),
            pltpu.VMEM((group, 2 * page_dev, rows), jnp.float32),
            pltpu.VMEM((128, rows), jnp.float32),
            pltpu.VMEM((128, rows), jnp.float32),
            pltpu.VMEM((heads, n_dev, block, hd), jnp.bfloat16),
            pltpu.VMEM((heads, n_dev, block, hd), jnp.bfloat16),
            pltpu.VMEM((n_dev, 2 * here, 128), jnp.float32),
            pltpu.VMEM((n_dev, 2 * here, 128), jnp.float32),
            pltpu.SemaphoreType.DMA((2,)),
            pltpu.SemaphoreType.DMA((heads + 1,)),
            pltpu.SemaphoreType.DMA((heads + 1,)),
            pltpu.SemaphoreType.DMA((heads + 1, n_dev)),
            pltpu.SemaphoreType.DMA((heads + 1, n_dev)),
        ],
        compiler_params=pltpu.CompilerParams(
            collective_id=0, has_side_effects=True, vmem_limit_bytes=40 * 1024 * 1024
        ),
    )(ids, lengths.reshape(1, rows), pos, sel, own, own_v, queries, kv)


def choose(token_kv, positions, page_owner, queries, own_kv, selected, lengths):
    rows_here = queries.shape[0] // (2 * lax.axis_size("seq"))
    run = direct_body if rows_here == 8 else body
    return run(token_kv, positions, page_owner, queries, own_kv, selected, lengths)


def solution(mesh):
    in_specs = (
        P("role", ("groups", "seq"), None, None),
        P("role", ("groups", "seq")),
        P(("groups", "seq")),
        P("groups", None),
        P("groups", None, None),
        P("groups", None, None),
        P("groups"),
    )
    out_specs = (P(("groups", "role", "seq"), None), P(("groups", "role", "seq"), None))
    return jax.shard_map(choose, mesh=mesh, in_specs=in_specs, out_specs=out_specs, check_vma=False)
```

```python
import functools
import math

import jax
import jax.numpy as jnp
from jax import lax
from jax.experimental import pallas as pl
from jax.experimental.pallas import tpu as pltpu
from jax.sharding import PartitionSpec as P

NEG = -1e30
LOG2E = 1.4426950408889634
MESH = pl.DeviceIdType.MESH


def from_behind(block, axis, distance):
    devices = range(lax.axis_size(axis))
    route = [(i - distance, i) for i in devices if i - distance in devices]
    return lax.ppermute(block, axis, route)


def owner_rank(owners):
    page_total = owners.shape[0]
    same_owner = owners[:, None] == owners[None, :]
    earlier = jnp.arange(page_total)[None, :] < jnp.arange(page_total)[:, None]
    return jnp.sum(same_owner & earlier, axis=1)


def pack_pages(target, slot_total, flat_kv, flat_sum, page_pos):
    chosen = jnp.arange(slot_total, dtype=jnp.int32)[:, None] == target[None, :]
    onehot = chosen.astype(jnp.bfloat16)
    sent_kv = jnp.dot(onehot, flat_kv, preferred_element_type=jnp.float32).astype(jnp.bfloat16)
    sent_sum = jnp.dot(onehot, flat_sum, preferred_element_type=jnp.float32).astype(jnp.bfloat16)
    sent_pos = jnp.sum(jnp.where(chosen[:, :, None], page_pos[None], 0), axis=1)
    return (sent_kv, sent_sum, sent_pos)


def attend(pool_kv, pool_sum, pool_pos, pool_ids, queries, selected, lengths, kv_heads):
    pool_total, page_len = pool_pos.shape
    kv_width = pool_kv.shape[-1]
    head_dim = kv_width // kv_heads
    row_total = queries.shape[0]
    group_size = queries.shape[1] // kv_width
    score_scale = 1.0 / math.sqrt(head_dim)
    token_total = pool_total * page_len
    row_block = 32
    block_count = row_total // row_block
    key_heads = jnp.transpose(
        pool_kv[:, :, 0, :].reshape(token_total, kv_heads, head_dim), (1, 0, 2)
    )
    value_heads = jnp.transpose(
        pool_kv[:, :, 1, :].reshape(token_total, kv_heads, head_dim), (1, 0, 2)
    )
    summary_heads = jnp.transpose(pool_sum.reshape(pool_total, 2, kv_heads, head_dim), (2, 0, 1, 3))
    timely = (pool_pos[None] < lengths[:, None, None]).reshape(
        block_count, row_block, pool_total, page_len
    )
    query_heads = jnp.transpose(
        queries.reshape(row_total, kv_heads, group_size, head_dim), (1, 0, 2, 3)
    )
    chosen_heads = jnp.transpose(selected, (1, 0, 2))

    def one_head(inputs):
        key_rows, value_rows, summary, query_head, chosen = inputs
        query_blocks = query_head.reshape(block_count, row_block, group_size, head_dim)
        chosen_blocks = chosen.reshape(block_count, row_block, chosen.shape[-1])

        def one_block(parts):
            query_block, chosen_block, timely_block = parts
            matches = chosen_block[:, :, None] == pool_ids[None, None, :]
            picked = jnp.any(matches, axis=1)
            usable = (picked[:, :, None] & timely_block).reshape(row_block, token_total)
            scores = (
                jnp.einsum("rgd,td->rgt", query_block, key_rows, preferred_element_type=jnp.float32)
                * score_scale
            )
            masked = jnp.where(usable[:, None, :], scores, NEG)
            largest = jnp.max(masked, axis=2)
            weights = jnp.where(usable[:, None, :], jnp.exp(masked - largest[:, :, None]), 0.0)
            totals = jnp.sum(weights, axis=2)
            sums = jnp.einsum(
                "rgt,td->rgd",
                weights.astype(jnp.bfloat16),
                value_rows,
                preferred_element_type=jnp.float32,
            )
            upper_part = jnp.maximum(query_block, 0)
            lower_part = jnp.maximum(-query_block, 0)
            upper_bound = jnp.einsum(
                "rgd,qd->rgq", upper_part, summary[:, 0], preferred_element_type=jnp.float32
            )
            upper_bound = (
                upper_bound
                - jnp.einsum(
                    "rgd,qd->rgq", lower_part, summary[:, 1], preferred_element_type=jnp.float32
                )
            ) * score_scale
            bound = jnp.einsum(
                "mfp,mlp->mlf",
                matches.astype(jnp.float32),
                upper_bound,
                precision=lax.Precision.HIGHEST,
            )
            return (largest, totals, sums, bound)

        largest, totals, sums, bound = lax.map(one_block, (query_blocks, chosen_blocks, timely))
        return (
            largest.reshape(row_total, group_size),
            totals.reshape(row_total, group_size),
            sums.reshape(row_total, group_size, head_dim),
            bound.reshape(row_total, group_size, -1),
        )

    largest, totals, sums, bounds = lax.map(
        one_head, (key_heads, value_heads, summary_heads, query_heads, chosen_heads)
    )
    largest = jnp.transpose(largest, (1, 0, 2)).reshape(row_total, kv_heads * group_size)
    totals = jnp.transpose(totals, (1, 0, 2)).reshape(row_total, kv_heads * group_size)
    sums = jnp.transpose(sums, (1, 0, 2, 3)).reshape(row_total, kv_heads * group_size, head_dim)
    bounds = jnp.transpose(bounds, (1, 0, 2, 3)).reshape(row_total, kv_heads * group_size, -1)
    return (largest, totals, sums, bounds)


def body(token_kv, positions, page_owner, queries, own_kv, selected, lengths):
    seq_total = lax.axis_size("seq")
    role_index = lax.axis_index("role")
    seq_index = lax.axis_index("seq")
    decoding = role_index == 1
    page_dev = page_owner.shape[0]
    tokens_dev = token_kv.shape[1]
    kv_width = token_kv.shape[3]
    page_len = tokens_dev // page_dev
    kv_heads = selected.shape[1]
    slot_count = max(2, 4 * page_dev // seq_total)
    inbound = seq_total * slot_count
    pool_dev = inbound + page_dev
    local_kv = token_kv[0].reshape(page_dev, page_len, 2, kv_width)
    local_pos = positions[0].reshape(page_dev, page_len)
    local_keys = local_kv[:, :, 0, :]
    local_sum = jnp.stack([jnp.max(local_keys, axis=1), jnp.min(local_keys, axis=1)], axis=1)
    order_rank = owner_rank(page_owner)
    flat_kv = local_kv.reshape(page_dev, page_len * 2 * kv_width)
    flat_sum = local_sum.reshape(page_dev, 2 * kv_width)
    out_kv, out_sum, out_pos = pack_pages(
        page_owner * slot_count + order_rank, inbound, flat_kv, flat_sum, local_pos
    )
    routed_kv, routed_sum, routed_pos = (
        lax.all_to_all(out_kv, "seq", split_axis=0, concat_axis=0, tiled=True),
        lax.all_to_all(out_sum, "seq", split_axis=0, concat_axis=0, tiled=True),
        lax.all_to_all(out_pos, "seq", split_axis=0, concat_axis=0, tiled=True),
    )
    got_kv, got_sum, got_pos = from_behind((routed_kv, routed_sum, routed_pos), "role", 1)
    pool_kv = jnp.concatenate([got_kv.reshape(inbound, page_len, 2, kv_width), local_kv], axis=0)
    pool_sum = jnp.concatenate([got_sum.reshape(inbound, 2, kv_width), local_sum], axis=0)
    pool_pos = jnp.concatenate([got_pos, local_pos], axis=0)
    pool_ids = jnp.where(decoding, seq_index * pool_dev + jnp.arange(pool_dev, dtype=jnp.int32), -1)
    largest, totals, sums, bounds = attend(
        pool_kv, pool_sum, pool_pos, pool_ids, queries, selected, lengths, kv_heads
    )
    row_total = queries.shape[0]
    device_total = 2 * seq_total
    rows_here = row_total // device_total
    first_row = (role_index * seq_total + seq_index) * rows_here
    overall = lax.pmax(largest, ("role", "seq"))
    factor = jnp.exp(largest - overall)
    sums, totals, bounds = (
        lax.psum_scatter(
            sums * factor[..., None], ("role", "seq"), scatter_dimension=0, tiled=True
        ),
        lax.psum_scatter(totals * factor, ("role", "seq"), scatter_dimension=0, tiled=True),
        lax.psum_scatter(bounds, ("role", "seq"), scatter_dimension=0, tiled=True),
    )
    largest = lax.dynamic_slice_in_dim(overall, first_row, rows_here, 0)
    head_dim = kv_width // kv_heads
    group_size = queries.shape[1] // kv_width
    score_scale = 1.0 / math.sqrt(head_dim)
    my_queries = lax.dynamic_slice_in_dim(queries, first_row, rows_here, 0).reshape(
        rows_here, kv_heads, group_size, head_dim
    )
    my_own = lax.dynamic_slice_in_dim(own_kv, first_row, rows_here, 0)
    own_keys = my_own[:, 0].reshape(rows_here, kv_heads, head_dim)
    own_values = my_own[:, 1].reshape(rows_here, kv_heads, 1, head_dim).astype(jnp.float32)
    own_score = (
        jnp.einsum(
            "rhgd,rhd->rhg", my_queries, own_keys, preferred_element_type=jnp.float32
        ).reshape(rows_here, kv_heads * group_size)
        * score_scale
    )
    highest = jnp.maximum(largest, own_score)
    fading = jnp.exp(largest - highest)
    fresh_weight = jnp.exp(own_score - highest)
    value_share = jnp.broadcast_to(own_values, (rows_here, kv_heads, group_size, head_dim)).reshape(
        rows_here, kv_heads * group_size, head_dim
    )
    attended = (sums * fading[..., None] + fresh_weight[..., None] * value_share) / (
        totals * fading + fresh_weight
    )[..., None]
    return (attended.reshape(rows_here, -1).astype(jnp.bfloat16), bounds.reshape(rows_here, -1))


def exchange_kernel(
    n_seq,
    heads,
    group,
    scale,
    slot_count,
    col_ref,
    row_ref,
    lens_ref,
    pos_ref,
    sel_ref,
    ownk_ref,
    ownv_ref,
    q_hbm,
    kv_hbm,
    att_ref,
    bnd_ref,
    q_buf,
    q_mine,
    kv_own,
    kv_got,
    pos_got,
    ids_buf,
    vt_buf,
    s_buf,
    p_buf,
    bias_buf,
    u_buf,
    mt_buf,
    keep_buf,
    keep_ml,
    y_send,
    y_recv,
    yml_send,
    yml_recv,
    z_send,
    z_recv,
    ml_send,
    ml_recv,
    load_sem,
    kv_ssem,
    kv_rsem,
    y_ssem,
    y_rsem,
    z_ssem,
    z_rsem,
):
    role = lax.axis_index("role")
    seq = lax.axis_index("seq")
    y = seq % 2
    z = seq // 2
    n_z = n_seq // 2
    n_same = 2 * n_z
    me = role * n_z + z
    mate = {"role": 1 - role, "seq": seq}
    beside = {"role": role, "seq": z * 2 + 1 - y}
    toks = kv_own.shape[2]
    hd = kv_own.shape[3]
    pages = toks // 16
    rows = q_buf.shape[0]
    here = rows // (2 * n_seq)
    half = q_buf.shape[1]
    pairs = group // 2
    n_sel = sel_ref.shape[1]

    def place_of(t):
        return {"role": t // n_z, "seq": (t % n_z) * 2 + y}

    q_copy = pltpu.make_async_copy(
        q_hbm.at[:, pl.ds(pl.multiple_of(role * half, half), half)], q_buf, load_sem.at[0]
    )
    q_copy.start()
    mine_at = pl.multiple_of(me * 2 * here, 2 * here)
    mine_copy = pltpu.make_async_copy(
        q_hbm.at[pl.ds(mine_at, 2 * here), :], q_mine, load_sem.at[1]
    )
    mine_copy.start()

    def own_copy(hl):
        at = pl.multiple_of((role * heads + hl) * hd, hd)
        return pltpu.make_async_copy(
            kv_hbm.at[:, :, pl.ds(at, hd)], kv_own.at[hl], load_sem.at[2 + hl]
        )

    for hl in range(heads):
        own_copy(hl).start()

    barrier = pltpu.get_barrier_semaphore()

    def greet(j, carry):
        t = lax.rem(me + j, n_same)
        pl.semaphore_signal(barrier, inc=1, device_id=place_of(t), device_id_type=MESH)
        return carry

    lax.fori_loop(1, n_same, greet, 0)
    pl.semaphore_signal(barrier, inc=1, device_id=beside, device_id_type=MESH)
    pl.semaphore_wait(barrier, n_same)

    def mate_copy(hl):
        at = pl.multiple_of(((1 - role) * heads + hl) * hd, hd)
        return pltpu.make_async_remote_copy(
            src_ref=kv_hbm.at[:, :, pl.ds(at, hd)],
            dst_ref=kv_got.at[hl],
            send_sem=kv_ssem.at[hl],
            recv_sem=kv_rsem.at[hl],
            device_id=mate,
            device_id_type=MESH,
        )

    pos_copy = pltpu.make_async_remote_copy(
        src_ref=pos_ref,
        dst_ref=pos_got,
        send_sem=kv_ssem.at[heads],
        recv_sem=kv_rsem.at[heads],
        device_id=mate,
        device_id_type=MESH,
    )
    pos_copy.start()
    for hl in range(heads):
        mate_copy(hl).start()

    col = col_ref[...]
    earlier = lax.broadcasted_iota(jnp.int32, (pages, pages), 1) < lax.broadcasted_iota(
        jnp.int32, (pages, pages), 0
    )
    same = (col[:, 0:pages] == row_ref[...]) & earlier
    rank = jnp.sum(jnp.where(same, 1.0, 0.0), axis=1, keepdims=True).astype(jnp.int32)
    inbound = n_seq * slot_count
    pool_dev = inbound + pages
    new_ids = col * pool_dev + seq * slot_count + rank
    old_ids = (
        lax.broadcasted_iota(jnp.int32, (pages, rows), 0) + seq * pool_dev + inbound
    )
    ids_buf[0:pages, :] = jnp.where(role == 0, new_ids, old_ids)
    ids_buf[pages : 2 * pages, :] = jnp.where(role == 0, old_ids, new_ids)
    mt_buf[...] = jnp.zeros_like(mt_buf)
    q_copy.wait()
    pos_copy.wait()

    def y_copy(hl):
        return pltpu.make_async_remote_copy(
            src_ref=y_send.at[hl],
            dst_ref=y_recv.at[hl],
            send_sem=y_ssem.at[0, hl],
            recv_sem=y_rsem.at[0, hl],
            device_id=beside,
            device_id_type=MESH,
        )

    def yml_copy(hl):
        return pltpu.make_async_remote_copy(
            src_ref=yml_send.at[hl],
            dst_ref=yml_recv.at[hl],
            send_sem=y_ssem.at[1, hl],
            recv_sem=y_rsem.at[1, hl],
            device_id=beside,
            device_id_type=MESH,
        )

    def z_copy(hl, t, slot):
        return pltpu.make_async_remote_copy(
            src_ref=z_send.at[hl, t],
            dst_ref=z_recv.at[hl, slot],
            send_sem=z_ssem.at[hl, t],
            recv_sem=z_rsem.at[hl, slot],
            device_id=place_of(t),
            device_id_type=MESH,
        )

    def ml_copy(t, slot):
        return pltpu.make_async_remote_copy(
            src_ref=ml_send.at[t],
            dst_ref=ml_recv.at[slot],
            send_sem=z_ssem.at[heads, t],
            recv_sem=z_rsem.at[heads, slot],
            device_id=place_of(t),
            device_id_type=MESH,
        )

    def split(first, second):
        count = first.shape[0]
        low = (lax.broadcasted_iota(jnp.int32, (count, rows), 1) // here) % 2 == 0
        zero = jnp.where(low, first, pltpu.roll(second, here, 1))
        one = jnp.where(low, pltpu.roll(first, rows - here, 1), second)
        return jnp.where(y == 0, zero, one), jnp.where(y == 0, one, zero)

    lens = lens_ref[...]
    dims = (((1,), (1,)), ((), ()))

    def merge(hl):
        y_copy(hl).wait()
        yml_copy(hl).wait()
        for gp in range(pairs):
            m1 = keep_ml[hl, gp : gp + 1, :]
            l1 = keep_ml[hl, pairs + gp : pairs + gp + 1, :]
            m2 = yml_recv[hl, gp : gp + 1, :]
            l2 = yml_recv[hl, pairs + gp : pairs + gp + 1, :]
            top = jnp.maximum(m1, m2)
            w1 = jnp.exp2(m1 - top) * l1
            w2 = jnp.exp2(m2 - top) * l2
            total = w1 + w2
            inv = 1.0 / total
            o = keep_buf[hl, gp, 0:hd, :] * (w1 * inv) + y_recv[hl, gp, 0:hd, :].astype(
                jnp.float32
            ) * (w2 * inv)
            z_send[hl, :, gp * 2 * here : (gp + 1) * 2 * here, :] = (
                o.T.reshape(n_same, 2 * here, hd).astype(jnp.bfloat16)
            )
            mt_buf[pl.ds(hl * pairs + gp, 1), :] = top
            mt_buf[pl.ds(64 + hl * pairs + gp, 1), :] = total
        bound = jnp.concatenate(
            [
                keep_buf[hl, gp, hd : hd + n_sel, :]
                + y_recv[hl, gp, hd : hd + n_sel, :].astype(jnp.float32)
                for gp in range(pairs)
            ],
            axis=0,
        )
        z_send[hl, :, group * here : (group + 2) * here, :] = (
            bound.T.reshape(n_same, 2 * here, hd).astype(jnp.bfloat16)
        )

        def go(j, carry):
            z_copy(hl, lax.rem(me + j, n_same), me).start()
            return carry

        lax.fori_loop(1, n_same, go, 0)
        z_recv[hl, me] = z_send[hl, me]

    def one_head(hl, carry):
        own_copy(hl).wait()
        mate_copy(hl).wait()
        sel = sel_ref[role * heads + hl]
        ids = ids_buf[...]
        hit = jnp.zeros((2 * pages, rows), jnp.float32) + NEG
        for s in range(n_sel):
            hit = jnp.where(ids == sel[s : s + 1, :], 0.0, hit)
        tops = []
        lows = []
        for part in range(2):
            start = (pos_ref if part == 0 else pos_got)[0:1, 0:1]
            left = lens - start
            wide = jnp.broadcast_to(
                hit[part * pages : (part + 1) * pages][:, None, :], (pages, 16, rows)
            ).reshape(toks, rows)
            place = lax.broadcasted_iota(jnp.int32, (toks, rows), 0)
            bias_buf[part * toks : (part + 1) * toks, :] = jnp.where(place < left, wide, NEG)
            block = kv_own if part == 0 else kv_got
            k32 = block[hl, 0].astype(jnp.float32).reshape(pages, 16, hd)
            tops.append(jnp.max(k32, axis=1))
            lows.append(jnp.min(k32, axis=1))
            v32 = block[hl, 1].astype(jnp.float32)
            vt_buf[:, part * toks : (part + 1) * toks] = v32.T.astype(jnp.bfloat16)
        summary = jnp.concatenate(
            [jnp.concatenate(tops, axis=0), jnp.concatenate(lows, axis=0)], axis=1
        ).astype(jnp.bfloat16)

        def one_pair(gp, carry):
            at = (hl * group + gp * 2) * hd
            q = jnp.concatenate(
                [
                    q_buf[:, pl.ds(pl.multiple_of(at, hd), hd)],
                    q_buf[:, pl.ds(pl.multiple_of(at + hd, hd), hd)],
                ],
                axis=0,
            )
            q32 = q.astype(jnp.float32)
            signed = jnp.concatenate(
                [jnp.maximum(q32, 0.0), jnp.minimum(q32, 0.0)], axis=1
            ).astype(jnp.bfloat16)
            u_buf[gp] = (
                lax.dot_general(summary, signed, dims, preferred_element_type=jnp.float32) * scale
            )
            for part in range(2):
                block = kv_own if part == 0 else kv_got
                bias = bias_buf[part * toks : (part + 1) * toks, :]
                s_buf[part * toks : (part + 1) * toks, :] = lax.dot_general(
                    block[hl, 0], q, dims, preferred_element_type=jnp.float32
                ) * (scale * LOG2E) + jnp.concatenate([bias, bias], axis=1)
            top = jnp.max(s_buf[...], axis=0, keepdims=True)
            w = jnp.exp2(s_buf[...] - top)
            total = jnp.sum(w, axis=0, keepdims=True)
            p_buf[...] = w.astype(jnp.bfloat16)
            o = jnp.dot(vt_buf[...], p_buf[...], preferred_element_type=jnp.float32)
            o = o * (1.0 / total)
            kept, sent = split(o[:, 0:rows], o[:, rows : 2 * rows])
            keep_buf[hl, gp, 0:hd, :] = kept
            y_send[hl, gp, 0:hd, :] = sent.astype(jnp.bfloat16)
            for stat, base in ((top, 0), (total, pairs)):
                stat = jnp.broadcast_to(stat, (8, 2 * rows))
                kept, sent = split(stat[:, 0:rows], stat[:, rows : 2 * rows])
                keep_ml[hl, pl.ds(base + gp, 1), :] = kept[0:1]
                yml_send[hl, pl.ds(base + gp, 1), :] = sent[0:1]
            return carry

        lax.fori_loop(0, pairs, one_pair, 0)

        acc = [jnp.zeros((n_sel, rows), jnp.float32) for _ in range(group)]
        for p in range(2 * pages):
            match = sel == ids_buf[p : p + 1, :]
            for g in range(group):
                at = (g % 2) * rows
                acc[g] = jnp.where(match, u_buf[g // 2, p : p + 1, at : at + rows], acc[g])
        for gp in range(pairs):
            kept, sent = split(acc[2 * gp], acc[2 * gp + 1])
            keep_buf[hl, gp, hd : hd + n_sel, :] = kept
            y_send[hl, gp, hd : hd + n_sel, :] = sent.astype(jnp.bfloat16)
        yml_copy(hl).start()
        y_copy(hl).start()

        @pl.when(hl > 0)
        def _():
            merge(hl - 1)

        return carry

    lax.fori_loop(0, heads, one_head, 0)
    merge(heads - 1)

    ml_send[...] = mt_buf[...].T.reshape(n_same, 2 * here, rows)

    def go_ml(j, carry):
        ml_copy(lax.rem(me + j, n_same), me).start()
        return carry

    lax.fori_loop(1, n_same, go_ml, 0)
    ml_recv[me] = ml_send[me]

    mine_copy.wait()
    lane = lax.broadcasted_iota(jnp.int32, (2 * here, rows), 1)
    fresh_scores = []
    for r in range(2):
        scores = jnp.zeros((2 * here, rows), jnp.float32)
        for hl in range(heads):
            h = r * heads + hl
            own_k = ownk_ref[:, h * hd : (h + 1) * hd]
            for gp in range(pairs):
                sums = []
                for sub in range(2):
                    at = (h * group + gp * 2 + sub) * hd
                    both = q_mine[:, at : at + hd].astype(jnp.float32)
                    one = jnp.where(y == 0, both[0:here], both[here : 2 * here])
                    sums.append(jnp.sum(one * own_k, axis=1, keepdims=True))
                scores = jnp.where(
                    lane == hl * pairs + gp, jnp.concatenate(sums, axis=0), scores
                )
        fresh_scores.append(scores * (scale * LOG2E))

    def end_ml(j, carry):
        t = lax.rem(me + j, n_same)
        ml_copy(t, t).wait()
        return carry

    lax.fori_loop(1, n_same, end_ml, 0)

    shares = []
    for r in range(2):
        mine = fresh_scores[r]
        stats = [ml_recv[r * n_z + c] for c in range(n_z)]
        highest = mine
        for m in stats:
            highest = jnp.maximum(highest, m)
        fresh = jnp.exp2(mine - highest)
        parts = [jnp.exp2(m - highest) * pltpu.roll(m, 64, 1) for m in stats]
        inv = fresh
        for w in parts:
            inv = inv + w
        inv = 1.0 / inv
        shares.append([w * inv for w in parts] + [fresh * inv])

    span = lax.broadcasted_iota(jnp.int32, (here, rows), 1) // n_sel
    for hl in range(heads):

        def end(j, carry):
            t = lax.rem(me + j, n_same)
            z_copy(hl, t, t).wait()
            return carry

        lax.fori_loop(1, n_same, end, 0)
        for r in range(2):
            h = r * heads + hl
            own_v = ownv_ref[:, h * hd : (h + 1) * hd]
            own_v = jnp.concatenate([own_v, own_v], axis=0)
            for gp in range(pairs):
                j = hl * pairs + gp
                total = shares[r][n_z][:, j : j + 1] * own_v
                for c in range(n_z):
                    block = z_recv[
                        hl, r * n_z + c, gp * 2 * here : (gp + 1) * 2 * here, :
                    ].astype(jnp.float32)
                    total = total + shares[r][c][:, j : j + 1] * block
                at = (h * group + gp * 2) * hd
                att_ref[:, at : at + hd] = total[0:here].astype(jnp.bfloat16)
                att_ref[:, at + hd : at + 2 * hd] = total[here : 2 * here].astype(jnp.bfloat16)
            bound = jnp.zeros((2 * here, hd), jnp.float32)
            for c in range(n_z):
                bound = bound + z_recv[
                    hl, r * n_z + c, group * here : (group + 2) * here, :
                ].astype(jnp.float32)
            a = bound[0:here]
            b = bound[here : 2 * here]
            at = h * group * n_sel
            bnd_ref[:, at : at + hd] = jnp.where(
                span == 0,
                a,
                jnp.where(
                    span == 1,
                    pltpu.roll(b, 32, 1),
                    jnp.where(span == 2, pltpu.roll(a, 32, 1), pltpu.roll(b, 64, 1)),
                ),
            )
            bnd_ref[:, at + hd : at + 2 * hd] = jnp.where(
                span == 0,
                pltpu.roll(a, 64, 1),
                jnp.where(
                    span == 1,
                    pltpu.roll(b, 96, 1),
                    jnp.where(span == 2, pltpu.roll(a, 96, 1), b),
                ),
            )


def direct_body(token_kv, positions, page_owner, queries, own_kv, selected, lengths):
    seq_total = lax.axis_size("seq")
    me = lax.axis_index("role") * seq_total + lax.axis_index("seq")
    page_dev = page_owner.shape[0]
    toks = token_kv.shape[1]
    kv_width = token_kv.shape[3]
    rows, kv_heads, n_sel = selected.shape
    hd = kv_width // kv_heads
    group = queries.shape[1] // kv_width
    heads = kv_heads // 2
    pairs = group // 2
    slot_count = max(2, 4 * page_dev // seq_total)
    n_same = seq_total
    here = rows // (2 * seq_total)

    col = jnp.broadcast_to(page_owner[:, None], (page_dev, rows))
    sel = jnp.transpose(selected, (1, 2, 0))
    kv = jnp.transpose(token_kv[0], (1, 0, 2))
    my_own = lax.dynamic_slice_in_dim(own_kv, me * here, here, 0).astype(jnp.float32)

    vmem = pl.BlockSpec(memory_space=pltpu.VMEM)
    hbm = pl.BlockSpec(memory_space=pl.ANY)
    block = (group + 2) * here
    f32 = jnp.float32
    bf16 = jnp.bfloat16
    return pl.pallas_call(
        functools.partial(
            exchange_kernel, seq_total, heads, group, 1.0 / math.sqrt(hd), slot_count
        ),
        out_shape=(
            jax.ShapeDtypeStruct((here, kv_heads * group * hd), bf16),
            jax.ShapeDtypeStruct((here, kv_heads * group * n_sel), f32),
        ),
        in_specs=[vmem] * 7 + [hbm] * 2,
        out_specs=(vmem, vmem),
        scratch_shapes=[
            pltpu.VMEM((rows, heads * group * hd), bf16),
            pltpu.VMEM((2 * here, kv_heads * group * hd), bf16),
            pltpu.VMEM((heads, 2, toks, hd), bf16),
            pltpu.VMEM((heads, 2, toks, hd), bf16),
            pltpu.VMEM((1, toks), jnp.int32),
            pltpu.VMEM((2 * page_dev, rows), jnp.int32),
            pltpu.VMEM((hd, 2 * toks), bf16),
            pltpu.VMEM((2 * toks, 2 * rows), f32),
            pltpu.VMEM((2 * toks, 2 * rows), bf16),
            pltpu.VMEM((2 * toks, rows), f32),
            pltpu.VMEM((pairs, 2 * page_dev, 2 * rows), f32),
            pltpu.VMEM((128, rows), f32),
            pltpu.VMEM((heads, pairs, hd + n_sel, rows), f32),
            pltpu.VMEM((heads, 2 * pairs, rows), f32),
            pltpu.VMEM((heads, pairs, hd + n_sel, rows), bf16),
            pltpu.VMEM((heads, pairs, hd + n_sel, rows), bf16),
            pltpu.VMEM((heads, 2 * pairs, rows), f32),
            pltpu.VMEM((heads, 2 * pairs, rows), f32),
            pltpu.VMEM((heads, n_same, block, hd), bf16),
            pltpu.VMEM((heads, n_same, block, hd), bf16),
            pltpu.VMEM((n_same, 2 * here, rows), f32),
            pltpu.VMEM((n_same, 2 * here, rows), f32),
            pltpu.SemaphoreType.DMA((heads + 2,)),
            pltpu.SemaphoreType.DMA((heads + 1,)),
            pltpu.SemaphoreType.DMA((heads + 1,)),
            pltpu.SemaphoreType.DMA((2, heads)),
            pltpu.SemaphoreType.DMA((2, heads)),
            pltpu.SemaphoreType.DMA((heads + 1, n_same)),
            pltpu.SemaphoreType.DMA((heads + 1, n_same)),
        ],
        compiler_params=pltpu.CompilerParams(
            collective_id=0, has_side_effects=True, vmem_limit_bytes=60 * 1024 * 1024
        ),
    )(
        col,
        page_owner.reshape(1, page_dev),
        lengths.reshape(1, rows),
        positions,
        sel,
        my_own[:, 0],
        my_own[:, 1],
        queries,
        kv,
    )


def choose(token_kv, positions, page_owner, queries, own_kv, selected, lengths):
    rows_here = queries.shape[0] // (2 * lax.axis_size("seq"))
    run = direct_body if rows_here == 8 else body
    return run(token_kv, positions, page_owner, queries, own_kv, selected, lengths)


def solution(mesh):
    in_specs = (
        P("role", ("groups", "seq"), None, None),
        P("role", ("groups", "seq")),
        P(("groups", "seq")),
        P("groups", None),
        P("groups", None, None),
        P("groups", None, None),
        P("groups"),
    )
    out_specs = (P(("groups", "role", "seq"), None), P(("groups", "role", "seq"), None))
    return jax.shard_map(choose, mesh=mesh, in_specs=in_specs, out_specs=out_specs, check_vma=False)
```

```python
import functools
import math

import jax
import jax.numpy as jnp
from jax import lax
from jax.experimental import pallas as pl
from jax.experimental.pallas import tpu as pltpu
from jax.sharding import PartitionSpec as P

NEG = -1e30
LOG2E = 1.4426950408889634
MESH = pl.DeviceIdType.MESH


def from_behind(block, axis, distance):
    devices = range(lax.axis_size(axis))
    route = [(i - distance, i) for i in devices if i - distance in devices]
    return lax.ppermute(block, axis, route)


def owner_rank(owners):
    page_total = owners.shape[0]
    same_owner = owners[:, None] == owners[None, :]
    earlier = jnp.arange(page_total)[None, :] < jnp.arange(page_total)[:, None]
    return jnp.sum(same_owner & earlier, axis=1)


def pack_pages(target, slot_total, flat_kv, flat_sum, page_pos):
    chosen = jnp.arange(slot_total, dtype=jnp.int32)[:, None] == target[None, :]
    onehot = chosen.astype(jnp.bfloat16)
    sent_kv = jnp.dot(onehot, flat_kv, preferred_element_type=jnp.float32).astype(jnp.bfloat16)
    sent_sum = jnp.dot(onehot, flat_sum, preferred_element_type=jnp.float32).astype(jnp.bfloat16)
    sent_pos = jnp.sum(jnp.where(chosen[:, :, None], page_pos[None], 0), axis=1)
    return (sent_kv, sent_sum, sent_pos)


def attend(pool_kv, pool_sum, pool_pos, pool_ids, queries, selected, lengths, kv_heads):
    pool_total, page_len = pool_pos.shape
    kv_width = pool_kv.shape[-1]
    head_dim = kv_width // kv_heads
    row_total = queries.shape[0]
    group_size = queries.shape[1] // kv_width
    score_scale = 1.0 / math.sqrt(head_dim)
    token_total = pool_total * page_len
    row_block = 32
    block_count = row_total // row_block
    key_heads = jnp.transpose(
        pool_kv[:, :, 0, :].reshape(token_total, kv_heads, head_dim), (1, 0, 2)
    )
    value_heads = jnp.transpose(
        pool_kv[:, :, 1, :].reshape(token_total, kv_heads, head_dim), (1, 0, 2)
    )
    summary_heads = jnp.transpose(pool_sum.reshape(pool_total, 2, kv_heads, head_dim), (2, 0, 1, 3))
    timely = (pool_pos[None] < lengths[:, None, None]).reshape(
        block_count, row_block, pool_total, page_len
    )
    query_heads = jnp.transpose(
        queries.reshape(row_total, kv_heads, group_size, head_dim), (1, 0, 2, 3)
    )
    chosen_heads = jnp.transpose(selected, (1, 0, 2))

    def one_head(inputs):
        key_rows, value_rows, summary, query_head, chosen = inputs
        query_blocks = query_head.reshape(block_count, row_block, group_size, head_dim)
        chosen_blocks = chosen.reshape(block_count, row_block, chosen.shape[-1])

        def one_block(parts):
            query_block, chosen_block, timely_block = parts
            matches = chosen_block[:, :, None] == pool_ids[None, None, :]
            picked = jnp.any(matches, axis=1)
            usable = (picked[:, :, None] & timely_block).reshape(row_block, token_total)
            scores = (
                jnp.einsum("rgd,td->rgt", query_block, key_rows, preferred_element_type=jnp.float32)
                * score_scale
            )
            masked = jnp.where(usable[:, None, :], scores, NEG)
            largest = jnp.max(masked, axis=2)
            weights = jnp.where(usable[:, None, :], jnp.exp(masked - largest[:, :, None]), 0.0)
            totals = jnp.sum(weights, axis=2)
            sums = jnp.einsum(
                "rgt,td->rgd",
                weights.astype(jnp.bfloat16),
                value_rows,
                preferred_element_type=jnp.float32,
            )
            upper_part = jnp.maximum(query_block, 0)
            lower_part = jnp.maximum(-query_block, 0)
            upper_bound = jnp.einsum(
                "rgd,qd->rgq", upper_part, summary[:, 0], preferred_element_type=jnp.float32
            )
            upper_bound = (
                upper_bound
                - jnp.einsum(
                    "rgd,qd->rgq", lower_part, summary[:, 1], preferred_element_type=jnp.float32
                )
            ) * score_scale
            bound = jnp.einsum(
                "mfp,mlp->mlf",
                matches.astype(jnp.float32),
                upper_bound,
                precision=lax.Precision.HIGHEST,
            )
            return (largest, totals, sums, bound)

        largest, totals, sums, bound = lax.map(one_block, (query_blocks, chosen_blocks, timely))
        return (
            largest.reshape(row_total, group_size),
            totals.reshape(row_total, group_size),
            sums.reshape(row_total, group_size, head_dim),
            bound.reshape(row_total, group_size, -1),
        )

    largest, totals, sums, bounds = lax.map(
        one_head, (key_heads, value_heads, summary_heads, query_heads, chosen_heads)
    )
    largest = jnp.transpose(largest, (1, 0, 2)).reshape(row_total, kv_heads * group_size)
    totals = jnp.transpose(totals, (1, 0, 2)).reshape(row_total, kv_heads * group_size)
    sums = jnp.transpose(sums, (1, 0, 2, 3)).reshape(row_total, kv_heads * group_size, head_dim)
    bounds = jnp.transpose(bounds, (1, 0, 2, 3)).reshape(row_total, kv_heads * group_size, -1)
    return (largest, totals, sums, bounds)


def body(token_kv, positions, page_owner, queries, own_kv, selected, lengths):
    seq_total = lax.axis_size("seq")
    role_index = lax.axis_index("role")
    seq_index = lax.axis_index("seq")
    decoding = role_index == 1
    page_dev = page_owner.shape[0]
    tokens_dev = token_kv.shape[1]
    kv_width = token_kv.shape[3]
    page_len = tokens_dev // page_dev
    kv_heads = selected.shape[1]
    slot_count = max(2, 4 * page_dev // seq_total)
    inbound = seq_total * slot_count
    pool_dev = inbound + page_dev
    local_kv = token_kv[0].reshape(page_dev, page_len, 2, kv_width)
    local_pos = positions[0].reshape(page_dev, page_len)
    local_keys = local_kv[:, :, 0, :]
    local_sum = jnp.stack([jnp.max(local_keys, axis=1), jnp.min(local_keys, axis=1)], axis=1)
    order_rank = owner_rank(page_owner)
    flat_kv = local_kv.reshape(page_dev, page_len * 2 * kv_width)
    flat_sum = local_sum.reshape(page_dev, 2 * kv_width)
    out_kv, out_sum, out_pos = pack_pages(
        page_owner * slot_count + order_rank, inbound, flat_kv, flat_sum, local_pos
    )
    routed_kv, routed_sum, routed_pos = (
        lax.all_to_all(out_kv, "seq", split_axis=0, concat_axis=0, tiled=True),
        lax.all_to_all(out_sum, "seq", split_axis=0, concat_axis=0, tiled=True),
        lax.all_to_all(out_pos, "seq", split_axis=0, concat_axis=0, tiled=True),
    )
    got_kv, got_sum, got_pos = from_behind((routed_kv, routed_sum, routed_pos), "role", 1)
    pool_kv = jnp.concatenate([got_kv.reshape(inbound, page_len, 2, kv_width), local_kv], axis=0)
    pool_sum = jnp.concatenate([got_sum.reshape(inbound, 2, kv_width), local_sum], axis=0)
    pool_pos = jnp.concatenate([got_pos, local_pos], axis=0)
    pool_ids = jnp.where(decoding, seq_index * pool_dev + jnp.arange(pool_dev, dtype=jnp.int32), -1)
    largest, totals, sums, bounds = attend(
        pool_kv, pool_sum, pool_pos, pool_ids, queries, selected, lengths, kv_heads
    )
    row_total = queries.shape[0]
    device_total = 2 * seq_total
    rows_here = row_total // device_total
    first_row = (role_index * seq_total + seq_index) * rows_here
    overall = lax.pmax(largest, ("role", "seq"))
    factor = jnp.exp(largest - overall)
    sums, totals, bounds = (
        lax.psum_scatter(
            sums * factor[..., None], ("role", "seq"), scatter_dimension=0, tiled=True
        ),
        lax.psum_scatter(totals * factor, ("role", "seq"), scatter_dimension=0, tiled=True),
        lax.psum_scatter(bounds, ("role", "seq"), scatter_dimension=0, tiled=True),
    )
    largest = lax.dynamic_slice_in_dim(overall, first_row, rows_here, 0)
    head_dim = kv_width // kv_heads
    group_size = queries.shape[1] // kv_width
    score_scale = 1.0 / math.sqrt(head_dim)
    my_queries = lax.dynamic_slice_in_dim(queries, first_row, rows_here, 0).reshape(
        rows_here, kv_heads, group_size, head_dim
    )
    my_own = lax.dynamic_slice_in_dim(own_kv, first_row, rows_here, 0)
    own_keys = my_own[:, 0].reshape(rows_here, kv_heads, head_dim)
    own_values = my_own[:, 1].reshape(rows_here, kv_heads, 1, head_dim).astype(jnp.float32)
    own_score = (
        jnp.einsum(
            "rhgd,rhd->rhg", my_queries, own_keys, preferred_element_type=jnp.float32
        ).reshape(rows_here, kv_heads * group_size)
        * score_scale
    )
    highest = jnp.maximum(largest, own_score)
    fading = jnp.exp(largest - highest)
    fresh_weight = jnp.exp(own_score - highest)
    value_share = jnp.broadcast_to(own_values, (rows_here, kv_heads, group_size, head_dim)).reshape(
        rows_here, kv_heads * group_size, head_dim
    )
    attended = (sums * fading[..., None] + fresh_weight[..., None] * value_share) / (
        totals * fading + fresh_weight
    )[..., None]
    return (attended.reshape(rows_here, -1).astype(jnp.bfloat16), bounds.reshape(rows_here, -1))


def exchange_kernel(
    n_seq,
    heads,
    group,
    scale,
    slot_count,
    row_ref,
    lens_ref,
    pos_ref,
    sel_ref,
    ownk_ref,
    ownv_ref,
    q_hbm,
    kv_hbm,
    att_ref,
    bnd_ref,
    q_buf,
    q_mine,
    kv_own,
    kv_got,
    pos_got,
    ids_buf,
    vt_buf,
    s_buf,
    p_buf,
    bias_buf,
    u_buf,
    mt_buf,
    keep_buf,
    keep_ml,
    y_send,
    y_recv,
    yml_send,
    yml_recv,
    z_send,
    z_recv,
    ml_send,
    ml_recv,
    load_sem,
    kv_ssem,
    kv_rsem,
    y_ssem,
    y_rsem,
    z_ssem,
    z_rsem,
):
    role = lax.axis_index("role")
    seq = lax.axis_index("seq")
    y = seq % 2
    z = seq // 2
    n_z = n_seq // 2
    n_same = 2 * n_z
    me = role * n_z + z
    mate = {"role": 1 - role, "seq": seq}
    beside = {"role": role, "seq": z * 2 + 1 - y}
    toks = kv_own.shape[2]
    hd = kv_own.shape[3]
    pages = toks // 16
    rows = q_buf.shape[0]
    here = rows // (2 * n_seq)
    half = q_buf.shape[1]
    pairs = group // 2
    n_sel = sel_ref.shape[1]

    def place_of(t):
        return {"role": t // n_z, "seq": (t % n_z) * 2 + y}

    q_copy = pltpu.make_async_copy(
        q_hbm.at[:, pl.ds(pl.multiple_of(role * half, half), half)], q_buf, load_sem.at[0]
    )
    q_copy.start()
    mine_at = pl.multiple_of(me * 2 * here, 2 * here)
    mine_copy = pltpu.make_async_copy(
        q_hbm.at[pl.ds(mine_at, 2 * here), :], q_mine, load_sem.at[1]
    )
    mine_copy.start()

    def own_copy(hl):
        at = pl.multiple_of((role * heads + hl) * hd, hd)
        return pltpu.make_async_copy(
            kv_hbm.at[:, :, pl.ds(at, hd)], kv_own.at[hl], load_sem.at[2 + hl]
        )

    for hl in range(heads):
        own_copy(hl).start()

    barrier = pltpu.get_barrier_semaphore()

    def greet(j, carry):
        t = lax.rem(me + j, n_same)
        pl.semaphore_signal(barrier, inc=1, device_id=place_of(t), device_id_type=MESH)
        return carry

    lax.fori_loop(1, n_same, greet, 0)
    pl.semaphore_signal(barrier, inc=1, device_id=beside, device_id_type=MESH)
    pl.semaphore_wait(barrier, n_same)

    def mate_copy(hl):
        at = pl.multiple_of(((1 - role) * heads + hl) * hd, hd)
        return pltpu.make_async_remote_copy(
            src_ref=kv_hbm.at[:, :, pl.ds(at, hd)],
            dst_ref=kv_got.at[hl],
            send_sem=kv_ssem.at[hl],
            recv_sem=kv_rsem.at[hl],
            device_id=mate,
            device_id_type=MESH,
        )

    pos_copy = pltpu.make_async_remote_copy(
        src_ref=pos_ref,
        dst_ref=pos_got,
        send_sem=kv_ssem.at[heads],
        recv_sem=kv_rsem.at[heads],
        device_id=mate,
        device_id_type=MESH,
    )
    pos_copy.start()
    for hl in range(heads):
        mate_copy(hl).start()

    lanes = lax.broadcasted_iota(jnp.int32, (pages, pages), 1)
    sublanes = lax.broadcasted_iota(jnp.int32, (pages, pages), 0)
    owners = jnp.broadcast_to(row_ref[...].astype(jnp.float32), (pages, pages))
    col = jnp.sum(jnp.where(lanes == sublanes, owners, 0.0), axis=1, keepdims=True)
    same = (col == owners) & (lanes < sublanes)
    col = jnp.broadcast_to(col, (pages, rows)).astype(jnp.int32)
    rank = jnp.sum(jnp.where(same, 1.0, 0.0), axis=1, keepdims=True).astype(jnp.int32)
    inbound = n_seq * slot_count
    pool_dev = inbound + pages
    new_ids = col * pool_dev + seq * slot_count + rank
    old_ids = (
        lax.broadcasted_iota(jnp.int32, (pages, rows), 0) + seq * pool_dev + inbound
    )
    ids_buf[0:pages, :] = jnp.where(role == 0, new_ids, old_ids)
    ids_buf[pages : 2 * pages, :] = jnp.where(role == 0, old_ids, new_ids)
    mt_buf[...] = jnp.zeros_like(mt_buf)
    q_copy.wait()
    pos_copy.wait()

    def y_copy(hl, gp):
        return pltpu.make_async_remote_copy(
            src_ref=y_send.at[hl, gp],
            dst_ref=y_recv.at[hl, gp],
            send_sem=y_ssem.at[gp, hl],
            recv_sem=y_rsem.at[gp, hl],
            device_id=beside,
            device_id_type=MESH,
        )

    def yml_copy(hl):
        return pltpu.make_async_remote_copy(
            src_ref=yml_send.at[hl],
            dst_ref=yml_recv.at[hl],
            send_sem=y_ssem.at[pairs, hl],
            recv_sem=y_rsem.at[pairs, hl],
            device_id=beside,
            device_id_type=MESH,
        )

    def z_copy(hl, t, slot):
        return pltpu.make_async_remote_copy(
            src_ref=z_send.at[hl, t],
            dst_ref=z_recv.at[hl, slot],
            send_sem=z_ssem.at[hl, t],
            recv_sem=z_rsem.at[hl, slot],
            device_id=place_of(t),
            device_id_type=MESH,
        )

    def ml_copy(t, slot):
        return pltpu.make_async_remote_copy(
            src_ref=ml_send.at[t],
            dst_ref=ml_recv.at[slot],
            send_sem=z_ssem.at[heads, t],
            recv_sem=z_rsem.at[heads, slot],
            device_id=place_of(t),
            device_id_type=MESH,
        )

    def split(first, second):
        count = first.shape[0]
        low = (lax.broadcasted_iota(jnp.int32, (count, rows), 1) // here) % 2 == 0
        zero = jnp.where(low, first, pltpu.roll(second, here, 1))
        one = jnp.where(low, pltpu.roll(first, rows - here, 1), second)
        return jnp.where(y == 0, zero, one), jnp.where(y == 0, one, zero)

    lens = lens_ref[...]
    dims = (((1,), (1,)), ((), ()))

    def merge(hl):
        yml_copy(hl).wait()
        for gp in range(pairs):
            y_copy(hl, gp).wait()
            m1 = keep_ml[hl, gp : gp + 1, :]
            l1 = keep_ml[hl, pairs + gp : pairs + gp + 1, :]
            m2 = yml_recv[hl, gp : gp + 1, :]
            l2 = yml_recv[hl, pairs + gp : pairs + gp + 1, :]
            top = jnp.maximum(m1, m2)
            w1 = jnp.exp2(m1 - top) * l1
            w2 = jnp.exp2(m2 - top) * l2
            total = w1 + w2
            inv = 1.0 / total
            o = keep_buf[hl, gp, 0:hd, :] * (w1 * inv) + y_recv[hl, gp, 0:hd, :].astype(
                jnp.float32
            ) * (w2 * inv)
            z_send[hl, :, gp * 2 * here : (gp + 1) * 2 * here, :] = (
                o.T.reshape(n_same, 2 * here, hd).astype(jnp.bfloat16)
            )
            mt_buf[pl.ds(hl * pairs + gp, 1), :] = top
            mt_buf[pl.ds(64 + hl * pairs + gp, 1), :] = total
        bound = jnp.concatenate(
            [
                keep_buf[hl, gp, hd : hd + n_sel, :]
                + y_recv[hl, gp, hd : hd + n_sel, :].astype(jnp.float32)
                for gp in range(pairs)
            ],
            axis=0,
        )
        z_send[hl, :, group * here : (group + 2) * here, :] = (
            bound.T.reshape(n_same, 2 * here, hd).astype(jnp.bfloat16)
        )

        def go(j, carry):
            z_copy(hl, lax.rem(me + j, n_same), me).start()
            return carry

        lax.fori_loop(1, n_same, go, 0)
        z_recv[hl, me] = z_send[hl, me]

    def one_head(hl, carry):
        own_copy(hl).wait()
        mate_copy(hl).wait()
        sel = sel_ref[role * heads + hl]
        ids = ids_buf[...]
        hit = jnp.zeros((2 * pages, rows), jnp.float32) + NEG
        for s in range(n_sel):
            hit = jnp.where(ids == sel[s : s + 1, :], 0.0, hit)
        tops = []
        lows = []
        for part in range(2):
            start = (pos_ref if part == 0 else pos_got)[0:1, 0:1]
            left = lens - start
            wide = jnp.broadcast_to(
                hit[part * pages : (part + 1) * pages][:, None, :], (pages, 16, rows)
            ).reshape(toks, rows)
            place = lax.broadcasted_iota(jnp.int32, (toks, rows), 0)
            bias_buf[part * toks : (part + 1) * toks, :] = jnp.where(place < left, wide, NEG)
            block = kv_own if part == 0 else kv_got
            k32 = block[hl, 0].astype(jnp.float32).reshape(pages, 16, hd)
            tops.append(jnp.max(k32, axis=1))
            lows.append(jnp.min(k32, axis=1))
            v32 = block[hl, 1].astype(jnp.float32)
            vt_buf[:, part * toks : (part + 1) * toks] = v32.T.astype(jnp.bfloat16)
        summary = jnp.concatenate(
            [jnp.concatenate(tops, axis=0), jnp.concatenate(lows, axis=0)], axis=1
        ).astype(jnp.bfloat16)

        def query(gp):
            at = (hl * group + gp * 2) * hd
            return jnp.concatenate(
                [
                    q_buf[:, pl.ds(pl.multiple_of(at, hd), hd)],
                    q_buf[:, pl.ds(pl.multiple_of(at + hd, hd), hd)],
                ],
                axis=0,
            )

        for gp in range(pairs):
            q32 = query(gp).astype(jnp.float32)
            signed = jnp.concatenate(
                [jnp.maximum(q32, 0.0), jnp.minimum(q32, 0.0)], axis=1
            ).astype(jnp.bfloat16)
            u_buf[gp] = (
                lax.dot_general(summary, signed, dims, preferred_element_type=jnp.float32) * scale
            )
        acc = [jnp.zeros((n_sel, rows), jnp.float32) for _ in range(group)]
        for p in range(2 * pages):
            match = sel == ids_buf[p : p + 1, :]
            for g in range(group):
                at = (g % 2) * rows
                acc[g] = jnp.where(match, u_buf[g // 2, p : p + 1, at : at + rows], acc[g])
        for gp in range(pairs):
            kept, sent = split(acc[2 * gp], acc[2 * gp + 1])
            keep_buf[hl, gp, hd : hd + n_sel, :] = kept
            y_send[hl, gp, hd : hd + n_sel, :] = sent.astype(jnp.bfloat16)

        @pl.when(hl > 0)
        def _():
            merge(hl - 1)

        step = toks // 2
        chunks = 4

        def score(gp):
            q = query(gp)
            top = None
            for ch in range(chunks):
                block = kv_own if ch < 2 else kv_got
                first = (ch % 2) * step
                bias = bias_buf[ch * step : (ch + 1) * step, :]
                part = lax.dot_general(
                    block[hl, 0, first : first + step, :],
                    q,
                    dims,
                    preferred_element_type=jnp.float32,
                ) * (scale * LOG2E) + jnp.concatenate([bias, bias], axis=1)
                s_buf[gp % 2, ch * step : (ch + 1) * step, :] = part
                high = jnp.max(part.reshape(step // 8, 8, 2 * rows), axis=0)
                top = high if top is None else jnp.maximum(top, high)
            return jnp.max(top, axis=0, keepdims=True)

        def attend_pair(gp, top):
            total = jnp.zeros((8, 2 * rows), jnp.float32)
            for ch in range(chunks):
                w = jnp.exp2(s_buf[gp % 2, ch * step : (ch + 1) * step, :] - top)
                total = total + jnp.sum(w.reshape(step // 8, 8, 2 * rows), axis=0)
                p_buf[gp % 2, ch * step : (ch + 1) * step, :] = w.astype(jnp.bfloat16)
            total = jnp.sum(total, axis=0, keepdims=True)
            o = jnp.dot(vt_buf[...], p_buf[gp % 2], preferred_element_type=jnp.float32)
            o = o * (1.0 / total)
            kept, sent = split(o[:, 0:rows], o[:, rows : 2 * rows])
            keep_buf[hl, gp, 0:hd, :] = kept
            y_send[hl, gp, 0:hd, :] = sent.astype(jnp.bfloat16)
            for stat, base in ((top, 0), (total, pairs)):
                stat = jnp.broadcast_to(stat, (8, 2 * rows))
                kept, sent = split(stat[:, 0:rows], stat[:, rows : 2 * rows])
                keep_ml[hl, base + gp : base + gp + 1, :] = kept[0:1]
                yml_send[hl, base + gp : base + gp + 1, :] = sent[0:1]
            y_copy(hl, gp).start()

        top = score(0)
        for gp in range(pairs):
            later = score(gp + 1) if gp + 1 < pairs else None
            attend_pair(gp, top)
            top = later
        yml_copy(hl).start()
        return carry

    lax.fori_loop(0, heads, one_head, 0)
    merge(heads - 1)

    ml_send[...] = mt_buf[...].T.reshape(n_same, 2 * here, rows)

    def go_ml(j, carry):
        ml_copy(lax.rem(me + j, n_same), me).start()
        return carry

    lax.fori_loop(1, n_same, go_ml, 0)
    ml_recv[me] = ml_send[me]

    mine_copy.wait()
    lane = lax.broadcasted_iota(jnp.int32, (2 * here, rows), 1)
    fresh_scores = []
    for r in range(2):
        scores = jnp.zeros((2 * here, rows), jnp.float32)
        for hl in range(heads):
            h = r * heads + hl
            own_k = ownk_ref[:, h * hd : (h + 1) * hd]
            for gp in range(pairs):
                sums = []
                for sub in range(2):
                    at = (h * group + gp * 2 + sub) * hd
                    both = q_mine[:, at : at + hd].astype(jnp.float32)
                    one = jnp.where(y == 0, both[0:here], both[here : 2 * here])
                    sums.append(jnp.sum(one * own_k, axis=1, keepdims=True))
                scores = jnp.where(
                    lane == hl * pairs + gp, jnp.concatenate(sums, axis=0), scores
                )
        fresh_scores.append(scores * (scale * LOG2E))

    def end_ml(j, carry):
        t = lax.rem(me + j, n_same)
        ml_copy(t, t).wait()
        return carry

    lax.fori_loop(1, n_same, end_ml, 0)

    shares = []
    for r in range(2):
        mine = fresh_scores[r]
        stats = [ml_recv[r * n_z + c] for c in range(n_z)]
        highest = mine
        for m in stats:
            highest = jnp.maximum(highest, m)
        fresh = jnp.exp2(mine - highest)
        parts = [jnp.exp2(m - highest) * pltpu.roll(m, 64, 1) for m in stats]
        inv = fresh
        for w in parts:
            inv = inv + w
        inv = 1.0 / inv
        shares.append([w * inv for w in parts] + [fresh * inv])

    span = lax.broadcasted_iota(jnp.int32, (here, rows), 1) // n_sel
    for hl in range(heads):

        def end(j, carry):
            t = lax.rem(me + j, n_same)
            z_copy(hl, t, t).wait()
            return carry

        lax.fori_loop(1, n_same, end, 0)
        for r in range(2):
            h = r * heads + hl
            own_v = ownv_ref[:, h * hd : (h + 1) * hd]
            own_v = jnp.concatenate([own_v, own_v], axis=0)
            for gp in range(pairs):
                j = hl * pairs + gp
                total = shares[r][n_z][:, j : j + 1] * own_v
                for c in range(n_z):
                    block = z_recv[
                        hl, r * n_z + c, gp * 2 * here : (gp + 1) * 2 * here, :
                    ].astype(jnp.float32)
                    total = total + shares[r][c][:, j : j + 1] * block
                at = (h * group + gp * 2) * hd
                att_ref[:, at : at + hd] = total[0:here].astype(jnp.bfloat16)
                att_ref[:, at + hd : at + 2 * hd] = total[here : 2 * here].astype(jnp.bfloat16)
            bound = jnp.zeros((2 * here, hd), jnp.float32)
            for c in range(n_z):
                bound = bound + z_recv[
                    hl, r * n_z + c, group * here : (group + 2) * here, :
                ].astype(jnp.float32)
            a = bound[0:here]
            b = bound[here : 2 * here]
            at = h * group * n_sel
            bnd_ref[:, at : at + hd] = jnp.where(
                span == 0,
                a,
                jnp.where(
                    span == 1,
                    pltpu.roll(b, 32, 1),
                    jnp.where(span == 2, pltpu.roll(a, 32, 1), pltpu.roll(b, 64, 1)),
                ),
            )
            bnd_ref[:, at + hd : at + 2 * hd] = jnp.where(
                span == 0,
                pltpu.roll(a, 64, 1),
                jnp.where(
                    span == 1,
                    pltpu.roll(b, 96, 1),
                    jnp.where(span == 2, pltpu.roll(a, 96, 1), b),
                ),
            )


def direct_body(token_kv, positions, page_owner, queries, own_kv, selected, lengths):
    seq_total = lax.axis_size("seq")
    me = lax.axis_index("role") * seq_total + lax.axis_index("seq")
    page_dev = page_owner.shape[0]
    toks = token_kv.shape[1]
    kv_width = token_kv.shape[3]
    rows, kv_heads, n_sel = selected.shape
    hd = kv_width // kv_heads
    group = queries.shape[1] // kv_width
    heads = kv_heads // 2
    pairs = group // 2
    slot_count = max(2, 4 * page_dev // seq_total)
    n_same = seq_total
    here = rows // (2 * seq_total)

    sel = jnp.transpose(selected, (1, 2, 0))
    kv = jnp.transpose(token_kv[0], (1, 0, 2))
    my_own = lax.dynamic_slice_in_dim(own_kv, me * here, here, 0).astype(jnp.float32)

    vmem = pl.BlockSpec(memory_space=pltpu.VMEM)
    hbm = pl.BlockSpec(memory_space=pl.ANY)
    block = (group + 2) * here
    f32 = jnp.float32
    bf16 = jnp.bfloat16
    return pl.pallas_call(
        functools.partial(
            exchange_kernel, seq_total, heads, group, 1.0 / math.sqrt(hd), slot_count
        ),
        out_shape=(
            jax.ShapeDtypeStruct((here, kv_heads * group * hd), bf16),
            jax.ShapeDtypeStruct((here, kv_heads * group * n_sel), f32),
        ),
        in_specs=[vmem] * 6 + [hbm] * 2,
        out_specs=(vmem, vmem),
        scratch_shapes=[
            pltpu.VMEM((rows, heads * group * hd), bf16),
            pltpu.VMEM((2 * here, kv_heads * group * hd), bf16),
            pltpu.VMEM((heads, 2, toks, hd), bf16),
            pltpu.VMEM((heads, 2, toks, hd), bf16),
            pltpu.VMEM((1, toks), jnp.int32),
            pltpu.VMEM((2 * page_dev, rows), jnp.int32),
            pltpu.VMEM((hd, 2 * toks), bf16),
            pltpu.VMEM((2, 2 * toks, 2 * rows), f32),
            pltpu.VMEM((2, 2 * toks, 2 * rows), bf16),
            pltpu.VMEM((2 * toks, rows), f32),
            pltpu.VMEM((pairs, 2 * page_dev, 2 * rows), f32),
            pltpu.VMEM((128, rows), f32),
            pltpu.VMEM((heads, pairs, hd + n_sel, rows), f32),
            pltpu.VMEM((heads, 2 * pairs, rows), f32),
            pltpu.VMEM((heads, pairs, hd + n_sel, rows), bf16),
            pltpu.VMEM((heads, pairs, hd + n_sel, rows), bf16),
            pltpu.VMEM((heads, 2 * pairs, rows), f32),
            pltpu.VMEM((heads, 2 * pairs, rows), f32),
            pltpu.VMEM((heads, n_same, block, hd), bf16),
            pltpu.VMEM((heads, n_same, block, hd), bf16),
            pltpu.VMEM((n_same, 2 * here, rows), f32),
            pltpu.VMEM((n_same, 2 * here, rows), f32),
            pltpu.SemaphoreType.DMA((heads + 2,)),
            pltpu.SemaphoreType.DMA((heads + 1,)),
            pltpu.SemaphoreType.DMA((heads + 1,)),
            pltpu.SemaphoreType.DMA((pairs + 1, heads)),
            pltpu.SemaphoreType.DMA((pairs + 1, heads)),
            pltpu.SemaphoreType.DMA((heads + 1, n_same)),
            pltpu.SemaphoreType.DMA((heads + 1, n_same)),
        ],
        compiler_params=pltpu.CompilerParams(
            collective_id=0, has_side_effects=True, vmem_limit_bytes=36 * 1024 * 1024
        ),
    )(
        page_owner.reshape(1, page_dev),
        lengths.reshape(1, rows),
        positions,
        sel,
        my_own[:, 0],
        my_own[:, 1],
        queries,
        kv,
    )


def choose(token_kv, positions, page_owner, queries, own_kv, selected, lengths):
    rows_here = queries.shape[0] // (2 * lax.axis_size("seq"))
    run = direct_body if rows_here == 8 else body
    return run(token_kv, positions, page_owner, queries, own_kv, selected, lengths)


def solution(mesh):
    in_specs = (
        P("role", ("groups", "seq"), None, None),
        P("role", ("groups", "seq")),
        P(("groups", "seq")),
        P("groups", None),
        P("groups", None, None),
        P("groups", None, None),
        P("groups"),
    )
    out_specs = (P(("groups", "role", "seq"), None), P(("groups", "role", "seq"), None))
    return jax.shard_map(choose, mesh=mesh, in_specs=in_specs, out_specs=out_specs, check_vma=False)
```

```python
import functools
import math

import jax
import jax.numpy as jnp
from jax import lax
from jax.experimental import pallas as pl
from jax.experimental.pallas import tpu as pltpu
from jax.sharding import PartitionSpec as P

NEG = -1e30
LOG2E = 1.4426950408889634
MESH = pl.DeviceIdType.MESH


def from_behind(block, axis, distance):
    devices = range(lax.axis_size(axis))
    route = [(i - distance, i) for i in devices if i - distance in devices]
    return lax.ppermute(block, axis, route)


def owner_rank(owners):
    page_total = owners.shape[0]
    same_owner = owners[:, None] == owners[None, :]
    earlier = jnp.arange(page_total)[None, :] < jnp.arange(page_total)[:, None]
    return jnp.sum(same_owner & earlier, axis=1)


def pack_pages(target, slot_total, flat_kv, flat_sum, page_pos):
    chosen = jnp.arange(slot_total, dtype=jnp.int32)[:, None] == target[None, :]
    onehot = chosen.astype(jnp.bfloat16)
    sent_kv = jnp.dot(onehot, flat_kv, preferred_element_type=jnp.float32).astype(jnp.bfloat16)
    sent_sum = jnp.dot(onehot, flat_sum, preferred_element_type=jnp.float32).astype(jnp.bfloat16)
    sent_pos = jnp.sum(jnp.where(chosen[:, :, None], page_pos[None], 0), axis=1)
    return (sent_kv, sent_sum, sent_pos)


def attend(pool_kv, pool_sum, pool_pos, pool_ids, queries, selected, lengths, kv_heads):
    pool_total, page_len = pool_pos.shape
    kv_width = pool_kv.shape[-1]
    head_dim = kv_width // kv_heads
    row_total = queries.shape[0]
    group_size = queries.shape[1] // kv_width
    score_scale = 1.0 / math.sqrt(head_dim)
    token_total = pool_total * page_len
    row_block = 32
    block_count = row_total // row_block
    key_heads = jnp.transpose(
        pool_kv[:, :, 0, :].reshape(token_total, kv_heads, head_dim), (1, 0, 2)
    )
    value_heads = jnp.transpose(
        pool_kv[:, :, 1, :].reshape(token_total, kv_heads, head_dim), (1, 0, 2)
    )
    summary_heads = jnp.transpose(pool_sum.reshape(pool_total, 2, kv_heads, head_dim), (2, 0, 1, 3))
    timely = (pool_pos[None] < lengths[:, None, None]).reshape(
        block_count, row_block, pool_total, page_len
    )
    query_heads = jnp.transpose(
        queries.reshape(row_total, kv_heads, group_size, head_dim), (1, 0, 2, 3)
    )
    chosen_heads = jnp.transpose(selected, (1, 0, 2))

    def one_head(inputs):
        key_rows, value_rows, summary, query_head, chosen = inputs
        query_blocks = query_head.reshape(block_count, row_block, group_size, head_dim)
        chosen_blocks = chosen.reshape(block_count, row_block, chosen.shape[-1])

        def one_block(parts):
            query_block, chosen_block, timely_block = parts
            matches = chosen_block[:, :, None] == pool_ids[None, None, :]
            picked = jnp.any(matches, axis=1)
            usable = (picked[:, :, None] & timely_block).reshape(row_block, token_total)
            scores = (
                jnp.einsum("rgd,td->rgt", query_block, key_rows, preferred_element_type=jnp.float32)
                * score_scale
            )
            masked = jnp.where(usable[:, None, :], scores, NEG)
            largest = jnp.max(masked, axis=2)
            weights = jnp.where(usable[:, None, :], jnp.exp(masked - largest[:, :, None]), 0.0)
            totals = jnp.sum(weights, axis=2)
            sums = jnp.einsum(
                "rgt,td->rgd",
                weights.astype(jnp.bfloat16),
                value_rows,
                preferred_element_type=jnp.float32,
            )
            upper_part = jnp.maximum(query_block, 0)
            lower_part = jnp.maximum(-query_block, 0)
            upper_bound = jnp.einsum(
                "rgd,qd->rgq", upper_part, summary[:, 0], preferred_element_type=jnp.float32
            )
            upper_bound = (
                upper_bound
                - jnp.einsum(
                    "rgd,qd->rgq", lower_part, summary[:, 1], preferred_element_type=jnp.float32
                )
            ) * score_scale
            bound = jnp.einsum(
                "mfp,mlp->mlf",
                matches.astype(jnp.float32),
                upper_bound,
                precision=lax.Precision.HIGHEST,
            )
            return (largest, totals, sums, bound)

        largest, totals, sums, bound = lax.map(one_block, (query_blocks, chosen_blocks, timely))
        return (
            largest.reshape(row_total, group_size),
            totals.reshape(row_total, group_size),
            sums.reshape(row_total, group_size, head_dim),
            bound.reshape(row_total, group_size, -1),
        )

    largest, totals, sums, bounds = lax.map(
        one_head, (key_heads, value_heads, summary_heads, query_heads, chosen_heads)
    )
    largest = jnp.transpose(largest, (1, 0, 2)).reshape(row_total, kv_heads * group_size)
    totals = jnp.transpose(totals, (1, 0, 2)).reshape(row_total, kv_heads * group_size)
    sums = jnp.transpose(sums, (1, 0, 2, 3)).reshape(row_total, kv_heads * group_size, head_dim)
    bounds = jnp.transpose(bounds, (1, 0, 2, 3)).reshape(row_total, kv_heads * group_size, -1)
    return (largest, totals, sums, bounds)


def body(token_kv, positions, page_owner, queries, own_kv, selected, lengths):
    seq_total = lax.axis_size("seq")
    role_index = lax.axis_index("role")
    seq_index = lax.axis_index("seq")
    decoding = role_index == 1
    page_dev = page_owner.shape[0]
    tokens_dev = token_kv.shape[1]
    kv_width = token_kv.shape[3]
    page_len = tokens_dev // page_dev
    kv_heads = selected.shape[1]
    slot_count = max(2, 4 * page_dev // seq_total)
    inbound = seq_total * slot_count
    pool_dev = inbound + page_dev
    local_kv = token_kv[0].reshape(page_dev, page_len, 2, kv_width)
    local_pos = positions[0].reshape(page_dev, page_len)
    local_keys = local_kv[:, :, 0, :]
    local_sum = jnp.stack([jnp.max(local_keys, axis=1), jnp.min(local_keys, axis=1)], axis=1)
    order_rank = owner_rank(page_owner)
    flat_kv = local_kv.reshape(page_dev, page_len * 2 * kv_width)
    flat_sum = local_sum.reshape(page_dev, 2 * kv_width)
    out_kv, out_sum, out_pos = pack_pages(
        page_owner * slot_count + order_rank, inbound, flat_kv, flat_sum, local_pos
    )
    routed_kv, routed_sum, routed_pos = (
        lax.all_to_all(out_kv, "seq", split_axis=0, concat_axis=0, tiled=True),
        lax.all_to_all(out_sum, "seq", split_axis=0, concat_axis=0, tiled=True),
        lax.all_to_all(out_pos, "seq", split_axis=0, concat_axis=0, tiled=True),
    )
    got_kv, got_sum, got_pos = from_behind((routed_kv, routed_sum, routed_pos), "role", 1)
    pool_kv = jnp.concatenate([got_kv.reshape(inbound, page_len, 2, kv_width), local_kv], axis=0)
    pool_sum = jnp.concatenate([got_sum.reshape(inbound, 2, kv_width), local_sum], axis=0)
    pool_pos = jnp.concatenate([got_pos, local_pos], axis=0)
    pool_ids = jnp.where(decoding, seq_index * pool_dev + jnp.arange(pool_dev, dtype=jnp.int32), -1)
    largest, totals, sums, bounds = attend(
        pool_kv, pool_sum, pool_pos, pool_ids, queries, selected, lengths, kv_heads
    )
    row_total = queries.shape[0]
    device_total = 2 * seq_total
    rows_here = row_total // device_total
    first_row = (role_index * seq_total + seq_index) * rows_here
    overall = lax.pmax(largest, ("role", "seq"))
    factor = jnp.exp(largest - overall)
    sums, totals, bounds = (
        lax.psum_scatter(
            sums * factor[..., None], ("role", "seq"), scatter_dimension=0, tiled=True
        ),
        lax.psum_scatter(totals * factor, ("role", "seq"), scatter_dimension=0, tiled=True),
        lax.psum_scatter(bounds, ("role", "seq"), scatter_dimension=0, tiled=True),
    )
    largest = lax.dynamic_slice_in_dim(overall, first_row, rows_here, 0)
    head_dim = kv_width // kv_heads
    group_size = queries.shape[1] // kv_width
    score_scale = 1.0 / math.sqrt(head_dim)
    my_queries = lax.dynamic_slice_in_dim(queries, first_row, rows_here, 0).reshape(
        rows_here, kv_heads, group_size, head_dim
    )
    my_own = lax.dynamic_slice_in_dim(own_kv, first_row, rows_here, 0)
    own_keys = my_own[:, 0].reshape(rows_here, kv_heads, head_dim)
    own_values = my_own[:, 1].reshape(rows_here, kv_heads, 1, head_dim).astype(jnp.float32)
    own_score = (
        jnp.einsum(
            "rhgd,rhd->rhg", my_queries, own_keys, preferred_element_type=jnp.float32
        ).reshape(rows_here, kv_heads * group_size)
        * score_scale
    )
    highest = jnp.maximum(largest, own_score)
    fading = jnp.exp(largest - highest)
    fresh_weight = jnp.exp(own_score - highest)
    value_share = jnp.broadcast_to(own_values, (rows_here, kv_heads, group_size, head_dim)).reshape(
        rows_here, kv_heads * group_size, head_dim
    )
    attended = (sums * fading[..., None] + fresh_weight[..., None] * value_share) / (
        totals * fading + fresh_weight
    )[..., None]
    return (attended.reshape(rows_here, -1).astype(jnp.bfloat16), bounds.reshape(rows_here, -1))


def exchange_kernel(
    n_seq,
    heads,
    group,
    scale,
    slot_count,
    row_ref,
    lens_ref,
    pos_ref,
    sel_ref,
    ownk_ref,
    ownv_ref,
    q_hbm,
    kv_hbm,
    att_ref,
    bnd_ref,
    q_buf,
    q_mine,
    kv_own,
    kv_got,
    pos_got,
    ids_buf,
    vt_buf,
    s_buf,
    p_buf,
    bias_buf,
    u_buf,
    mt_buf,
    keep_buf,
    keep_ml,
    y_send,
    y_recv,
    yml_send,
    yml_recv,
    z_send,
    z_recv,
    ml_send,
    ml_recv,
    load_sem,
    kv_ssem,
    kv_rsem,
    y_ssem,
    y_rsem,
    z_ssem,
    z_rsem,
):
    role = lax.axis_index("role")
    seq = lax.axis_index("seq")
    y = seq % 2
    z = seq // 2
    n_z = n_seq // 2
    n_same = 2 * n_z
    me = role * n_z + z
    mate = {"role": 1 - role, "seq": seq}
    beside = {"role": role, "seq": z * 2 + 1 - y}
    toks = kv_own.shape[2]
    hd = kv_own.shape[3]
    pages = toks // 16
    rows = q_buf.shape[0]
    here = rows // (2 * n_seq)
    half = q_buf.shape[1]
    pairs = group // 2
    n_sel = sel_ref.shape[1]

    def place_of(t):
        return {"role": t // n_z, "seq": (t % n_z) * 2 + y}

    q_copy = pltpu.make_async_copy(
        q_hbm.at[:, pl.ds(pl.multiple_of(role * half, half), half)], q_buf, load_sem.at[0]
    )
    q_copy.start()
    mine_at = pl.multiple_of(me * 2 * here, 2 * here)
    mine_copy = pltpu.make_async_copy(
        q_hbm.at[pl.ds(mine_at, 2 * here), :], q_mine, load_sem.at[1]
    )
    mine_copy.start()

    def own_copy(hl):
        at = pl.multiple_of((role * heads + hl) * hd, hd)
        return pltpu.make_async_copy(
            kv_hbm.at[:, :, pl.ds(at, hd)], kv_own.at[hl], load_sem.at[2 + hl]
        )

    for hl in range(heads):
        own_copy(hl).start()

    barrier = pltpu.get_barrier_semaphore()

    def greet(j, carry):
        t = lax.rem(me + j, n_same)
        pl.semaphore_signal(barrier, inc=1, device_id=place_of(t), device_id_type=MESH)
        return carry

    lax.fori_loop(1, n_same, greet, 0)
    pl.semaphore_signal(barrier, inc=1, device_id=beside, device_id_type=MESH)
    pl.semaphore_wait(barrier, n_same)

    def mate_copy(hl):
        at = pl.multiple_of(((1 - role) * heads + hl) * hd, hd)
        return pltpu.make_async_remote_copy(
            src_ref=kv_hbm.at[:, :, pl.ds(at, hd)],
            dst_ref=kv_got.at[hl],
            send_sem=kv_ssem.at[hl],
            recv_sem=kv_rsem.at[hl],
            device_id=mate,
            device_id_type=MESH,
        )

    pos_copy = pltpu.make_async_remote_copy(
        src_ref=pos_ref,
        dst_ref=pos_got,
        send_sem=kv_ssem.at[heads],
        recv_sem=kv_rsem.at[heads],
        device_id=mate,
        device_id_type=MESH,
    )
    pos_copy.start()
    for hl in range(heads):
        mate_copy(hl).start()

    lanes = lax.broadcasted_iota(jnp.int32, (pages, pages), 1)
    sublanes = lax.broadcasted_iota(jnp.int32, (pages, pages), 0)
    owners = jnp.broadcast_to(row_ref[...].astype(jnp.float32), (pages, pages))
    col = jnp.sum(jnp.where(lanes == sublanes, owners, 0.0), axis=1, keepdims=True)
    same = (col == owners) & (lanes < sublanes)
    col = jnp.broadcast_to(col, (pages, rows)).astype(jnp.int32)
    rank = jnp.sum(jnp.where(same, 1.0, 0.0), axis=1, keepdims=True).astype(jnp.int32)
    inbound = n_seq * slot_count
    pool_dev = inbound + pages
    new_ids = col * pool_dev + seq * slot_count + rank
    old_ids = (
        lax.broadcasted_iota(jnp.int32, (pages, rows), 0) + seq * pool_dev + inbound
    )
    ids_buf[0:pages, :] = jnp.where(role == 0, new_ids, old_ids)
    ids_buf[pages : 2 * pages, :] = jnp.where(role == 0, old_ids, new_ids)
    mt_buf[...] = jnp.zeros_like(mt_buf)
    q_copy.wait()
    pos_copy.wait()

    def y_copy(hl, gp):
        return pltpu.make_async_remote_copy(
            src_ref=y_send.at[hl, gp],
            dst_ref=y_recv.at[hl, gp],
            send_sem=y_ssem.at[gp, hl],
            recv_sem=y_rsem.at[gp, hl],
            device_id=beside,
            device_id_type=MESH,
        )

    def yml_copy(hl):
        return pltpu.make_async_remote_copy(
            src_ref=yml_send.at[hl],
            dst_ref=yml_recv.at[hl],
            send_sem=y_ssem.at[pairs, hl],
            recv_sem=y_rsem.at[pairs, hl],
            device_id=beside,
            device_id_type=MESH,
        )

    def z_copy(hl, t, slot):
        return pltpu.make_async_remote_copy(
            src_ref=z_send.at[hl, t],
            dst_ref=z_recv.at[hl, slot],
            send_sem=z_ssem.at[hl, t],
            recv_sem=z_rsem.at[hl, slot],
            device_id=place_of(t),
            device_id_type=MESH,
        )

    def ml_copy(t, slot):
        return pltpu.make_async_remote_copy(
            src_ref=ml_send.at[t],
            dst_ref=ml_recv.at[slot],
            send_sem=z_ssem.at[heads, t],
            recv_sem=z_rsem.at[heads, slot],
            device_id=place_of(t),
            device_id_type=MESH,
        )

    def split(first, second):
        count = first.shape[0]
        low = (lax.broadcasted_iota(jnp.int32, (count, rows), 1) // here) % 2 == 0
        zero = jnp.where(low, first, pltpu.roll(second, here, 1))
        one = jnp.where(low, pltpu.roll(first, rows - here, 1), second)
        return jnp.where(y == 0, zero, one), jnp.where(y == 0, one, zero)

    lens = lens_ref[...]
    dims = (((1,), (1,)), ((), ()))

    def merge(hl):
        yml_copy(hl).wait()
        for gp in range(pairs):
            y_copy(hl, gp).wait()
            m1 = keep_ml[hl, gp : gp + 1, :]
            l1 = keep_ml[hl, pairs + gp : pairs + gp + 1, :]
            m2 = yml_recv[hl, gp : gp + 1, :]
            l2 = yml_recv[hl, pairs + gp : pairs + gp + 1, :]
            top = jnp.maximum(m1, m2)
            w1 = jnp.exp2(m1 - top) * l1
            w2 = jnp.exp2(m2 - top) * l2
            total = w1 + w2
            inv = 1.0 / total
            o = keep_buf[hl, gp, 0:hd, :] * (w1 * inv) + y_recv[hl, gp, 0:hd, :].astype(
                jnp.float32
            ) * (w2 * inv)
            z_send[hl, :, gp * 2 * here : (gp + 1) * 2 * here, :] = (
                o.T.reshape(n_same, 2 * here, hd).astype(jnp.bfloat16)
            )
            mt_buf[pl.ds(hl * pairs + gp, 1), :] = top
            mt_buf[pl.ds(64 + hl * pairs + gp, 1), :] = total
        bound = jnp.concatenate(
            [
                keep_buf[hl, gp, hd : hd + n_sel, :]
                + y_recv[hl, gp, hd : hd + n_sel, :].astype(jnp.float32)
                for gp in range(pairs)
            ],
            axis=0,
        )
        z_send[hl, :, group * here : (group + 2) * here, :] = (
            bound.T.reshape(n_same, 2 * here, hd).astype(jnp.bfloat16)
        )

        def go(j, carry):
            z_copy(hl, lax.rem(me + j, n_same), me).start()
            return carry

        lax.fori_loop(1, n_same, go, 0)
        z_recv[hl, me] = z_send[hl, me]

    def one_head(hl, carry):
        own_copy(hl).wait()
        mate_copy(hl).wait()
        sel = sel_ref[role * heads + hl]
        ids = ids_buf[...]
        hit = jnp.zeros((2 * pages, rows), jnp.float32) + NEG
        for s in range(n_sel):
            hit = jnp.where(ids == sel[s : s + 1, :], 0.0, hit)
        tops = []
        lows = []
        for part in range(2):
            start = (pos_ref if part == 0 else pos_got)[0:1, 0:1]
            left = lens - start
            wide = jnp.broadcast_to(
                hit[part * pages : (part + 1) * pages][:, None, :], (pages, 16, rows)
            ).reshape(toks, rows)
            place = lax.broadcasted_iota(jnp.int32, (toks, rows), 0)
            bias_buf[part * toks : (part + 1) * toks, :] = jnp.where(place < left, wide, NEG)
            block = kv_own if part == 0 else kv_got
            k32 = block[hl, 0].astype(jnp.float32).reshape(pages, 16, hd)
            tops.append(jnp.max(k32, axis=1))
            lows.append(jnp.min(k32, axis=1))
            v32 = block[hl, 1].astype(jnp.float32)
            vt_buf[:, part * toks : (part + 1) * toks] = v32.T.astype(jnp.bfloat16)
        summary = jnp.concatenate(
            [jnp.concatenate(tops, axis=0), jnp.concatenate(lows, axis=0)], axis=1
        ).astype(jnp.bfloat16)

        def query(gp):
            at = (hl * group + gp * 2) * hd
            return jnp.concatenate(
                [
                    q_buf[:, pl.ds(pl.multiple_of(at, hd), hd)],
                    q_buf[:, pl.ds(pl.multiple_of(at + hd, hd), hd)],
                ],
                axis=0,
            )

        for gp in range(pairs):
            q32 = query(gp).astype(jnp.float32)
            signed = jnp.concatenate(
                [jnp.maximum(q32, 0.0), jnp.minimum(q32, 0.0)], axis=1
            ).astype(jnp.bfloat16)
            u_buf[gp] = (
                lax.dot_general(summary, signed, dims, preferred_element_type=jnp.float32) * scale
            )
        acc = [jnp.zeros((n_sel, rows), jnp.float32) for _ in range(group)]
        for p in range(2 * pages):
            match = sel == ids_buf[p : p + 1, :]
            for g in range(group):
                at = (g % 2) * rows
                acc[g] = jnp.where(match, u_buf[g // 2, p : p + 1, at : at + rows], acc[g])
        for gp in range(pairs):
            kept, sent = split(acc[2 * gp], acc[2 * gp + 1])
            keep_buf[hl, gp, hd : hd + n_sel, :] = kept
            y_send[hl, gp, hd : hd + n_sel, :] = sent.astype(jnp.bfloat16)

        step = toks // 2
        chunks = 4

        def score(gp):
            q = query(gp)
            top = None
            for ch in range(chunks):
                block = kv_own if ch < 2 else kv_got
                first = (ch % 2) * step
                bias = bias_buf[ch * step : (ch + 1) * step, :]
                part = lax.dot_general(
                    block[hl, 0, first : first + step, :],
                    q,
                    dims,
                    preferred_element_type=jnp.float32,
                ) * (scale * LOG2E) + jnp.concatenate([bias, bias], axis=1)
                s_buf[gp % 2, ch * step : (ch + 1) * step, :] = part
                high = jnp.max(part.reshape(step // 8, 8, 2 * rows), axis=0)
                top = high if top is None else jnp.maximum(top, high)
            return jnp.max(top, axis=0, keepdims=True)

        def attend_pair(gp, top):
            total = jnp.zeros((8, 2 * rows), jnp.float32)
            for ch in range(chunks):
                w = jnp.exp2(s_buf[gp % 2, ch * step : (ch + 1) * step, :] - top)
                total = total + jnp.sum(w.reshape(step // 8, 8, 2 * rows), axis=0)
                p_buf[gp % 2, ch * step : (ch + 1) * step, :] = w.astype(jnp.bfloat16)
            total = jnp.sum(total, axis=0, keepdims=True)
            o = jnp.dot(vt_buf[...], p_buf[gp % 2], preferred_element_type=jnp.float32)
            o = o * (1.0 / total)
            kept, sent = split(o[:, 0:rows], o[:, rows : 2 * rows])
            keep_buf[hl, gp, 0:hd, :] = kept
            y_send[hl, gp, 0:hd, :] = sent.astype(jnp.bfloat16)
            for stat, base in ((top, 0), (total, pairs)):
                stat = jnp.broadcast_to(stat, (8, 2 * rows))
                kept, sent = split(stat[:, 0:rows], stat[:, rows : 2 * rows])
                keep_ml[hl, base + gp : base + gp + 1, :] = kept[0:1]
                yml_send[hl, base + gp : base + gp + 1, :] = sent[0:1]
            y_copy(hl, gp).start()

        top = score(0)
        for gp in range(pairs):
            later = score(gp + 1) if gp + 1 < pairs else None
            attend_pair(gp, top)
            top = later
            if gp == pairs - 2:

                @pl.when(hl > 0)
                def _():
                    merge(hl - 1)

        yml_copy(hl).start()
        return carry

    lax.fori_loop(0, heads, one_head, 0)
    merge(heads - 1)

    ml_send[...] = mt_buf[...].T.reshape(n_same, 2 * here, rows)

    def go_ml(j, carry):
        ml_copy(lax.rem(me + j, n_same), me).start()
        return carry

    lax.fori_loop(1, n_same, go_ml, 0)
    ml_recv[me] = ml_send[me]

    mine_copy.wait()
    lane = lax.broadcasted_iota(jnp.int32, (2 * here, rows), 1)
    fresh_scores = []
    for r in range(2):
        scores = jnp.zeros((2 * here, rows), jnp.float32)
        for hl in range(heads):
            h = r * heads + hl
            own_k = ownk_ref[:, h * hd : (h + 1) * hd]
            for gp in range(pairs):
                sums = []
                for sub in range(2):
                    at = (h * group + gp * 2 + sub) * hd
                    both = q_mine[:, at : at + hd].astype(jnp.float32)
                    one = jnp.where(y == 0, both[0:here], both[here : 2 * here])
                    sums.append(jnp.sum(one * own_k, axis=1, keepdims=True))
                scores = jnp.where(
                    lane == hl * pairs + gp, jnp.concatenate(sums, axis=0), scores
                )
        fresh_scores.append(scores * (scale * LOG2E))

    def end_ml(j, carry):
        t = lax.rem(me + j, n_same)
        ml_copy(t, t).wait()
        return carry

    lax.fori_loop(1, n_same, end_ml, 0)

    shares = []
    for r in range(2):
        mine = fresh_scores[r]
        stats = [ml_recv[r * n_z + c] for c in range(n_z)]
        highest = mine
        for m in stats:
            highest = jnp.maximum(highest, m)
        fresh = jnp.exp2(mine - highest)
        parts = [jnp.exp2(m - highest) * pltpu.roll(m, 64, 1) for m in stats]
        inv = fresh
        for w in parts:
            inv = inv + w
        inv = 1.0 / inv
        shares.append([w * inv for w in parts] + [fresh * inv])

    span = lax.broadcasted_iota(jnp.int32, (here, rows), 1) // n_sel
    for hl in range(heads):

        def end(j, carry):
            t = lax.rem(me + j, n_same)
            z_copy(hl, t, t).wait()
            return carry

        lax.fori_loop(1, n_same, end, 0)
        for r in range(2):
            h = r * heads + hl
            own_v = ownv_ref[:, h * hd : (h + 1) * hd]
            own_v = jnp.concatenate([own_v, own_v], axis=0)
            for gp in range(pairs):
                j = hl * pairs + gp
                total = shares[r][n_z][:, j : j + 1] * own_v
                for c in range(n_z):
                    block = z_recv[
                        hl, r * n_z + c, gp * 2 * here : (gp + 1) * 2 * here, :
                    ].astype(jnp.float32)
                    total = total + shares[r][c][:, j : j + 1] * block
                at = (h * group + gp * 2) * hd
                att_ref[:, at : at + hd] = total[0:here].astype(jnp.bfloat16)
                att_ref[:, at + hd : at + 2 * hd] = total[here : 2 * here].astype(jnp.bfloat16)
            bound = jnp.zeros((2 * here, hd), jnp.float32)
            for c in range(n_z):
                bound = bound + z_recv[
                    hl, r * n_z + c, group * here : (group + 2) * here, :
                ].astype(jnp.float32)
            a = bound[0:here]
            b = bound[here : 2 * here]
            at = h * group * n_sel
            bnd_ref[:, at : at + hd] = jnp.where(
                span == 0,
                a,
                jnp.where(
                    span == 1,
                    pltpu.roll(b, 32, 1),
                    jnp.where(span == 2, pltpu.roll(a, 32, 1), pltpu.roll(b, 64, 1)),
                ),
            )
            bnd_ref[:, at + hd : at + 2 * hd] = jnp.where(
                span == 0,
                pltpu.roll(a, 64, 1),
                jnp.where(
                    span == 1,
                    pltpu.roll(b, 96, 1),
                    jnp.where(span == 2, pltpu.roll(a, 96, 1), b),
                ),
            )


def direct_body(token_kv, positions, page_owner, queries, own_kv, selected, lengths):
    seq_total = lax.axis_size("seq")
    me = lax.axis_index("role") * seq_total + lax.axis_index("seq")
    page_dev = page_owner.shape[0]
    toks = token_kv.shape[1]
    kv_width = token_kv.shape[3]
    rows, kv_heads, n_sel = selected.shape
    hd = kv_width // kv_heads
    group = queries.shape[1] // kv_width
    heads = kv_heads // 2
    pairs = group // 2
    slot_count = max(2, 4 * page_dev // seq_total)
    n_same = seq_total
    here = rows // (2 * seq_total)

    sel = jnp.transpose(selected, (1, 2, 0))
    kv = jnp.transpose(token_kv[0], (1, 0, 2))
    my_own = lax.dynamic_slice_in_dim(own_kv, me * here, here, 0).astype(jnp.float32)

    vmem = pl.BlockSpec(memory_space=pltpu.VMEM)
    hbm = pl.BlockSpec(memory_space=pl.ANY)
    block = (group + 2) * here
    f32 = jnp.float32
    bf16 = jnp.bfloat16
    return pl.pallas_call(
        functools.partial(
            exchange_kernel, seq_total, heads, group, 1.0 / math.sqrt(hd), slot_count
        ),
        out_shape=(
            jax.ShapeDtypeStruct((here, kv_heads * group * hd), bf16),
            jax.ShapeDtypeStruct((here, kv_heads * group * n_sel), f32),
        ),
        in_specs=[vmem] * 6 + [hbm] * 2,
        out_specs=(vmem, vmem),
        scratch_shapes=[
            pltpu.VMEM((rows, heads * group * hd), bf16),
            pltpu.VMEM((2 * here, kv_heads * group * hd), bf16),
            pltpu.VMEM((heads, 2, toks, hd), bf16),
            pltpu.VMEM((heads, 2, toks, hd), bf16),
            pltpu.VMEM((1, toks), jnp.int32),
            pltpu.VMEM((2 * page_dev, rows), jnp.int32),
            pltpu.VMEM((hd, 2 * toks), bf16),
            pltpu.VMEM((2, 2 * toks, 2 * rows), f32),
            pltpu.VMEM((2, 2 * toks, 2 * rows), bf16),
            pltpu.VMEM((2 * toks, rows), f32),
            pltpu.VMEM((pairs, 2 * page_dev, 2 * rows), f32),
            pltpu.VMEM((128, rows), f32),
            pltpu.VMEM((heads, pairs, hd + n_sel, rows), f32),
            pltpu.VMEM((heads, 2 * pairs, rows), f32),
            pltpu.VMEM((heads, pairs, hd + n_sel, rows), bf16),
            pltpu.VMEM((heads, pairs, hd + n_sel, rows), bf16),
            pltpu.VMEM((heads, 2 * pairs, rows), f32),
            pltpu.VMEM((heads, 2 * pairs, rows), f32),
            pltpu.VMEM((heads, n_same, block, hd), bf16),
            pltpu.VMEM((heads, n_same, block, hd), bf16),
            pltpu.VMEM((n_same, 2 * here, rows), f32),
            pltpu.VMEM((n_same, 2 * here, rows), f32),
            pltpu.SemaphoreType.DMA((heads + 2,)),
            pltpu.SemaphoreType.DMA((heads + 1,)),
            pltpu.SemaphoreType.DMA((heads + 1,)),
            pltpu.SemaphoreType.DMA((pairs + 1, heads)),
            pltpu.SemaphoreType.DMA((pairs + 1, heads)),
            pltpu.SemaphoreType.DMA((heads + 1, n_same)),
            pltpu.SemaphoreType.DMA((heads + 1, n_same)),
        ],
        compiler_params=pltpu.CompilerParams(
            collective_id=0, has_side_effects=True, vmem_limit_bytes=36 * 1024 * 1024
        ),
    )(
        page_owner.reshape(1, page_dev),
        lengths.reshape(1, rows),
        positions,
        sel,
        my_own[:, 0],
        my_own[:, 1],
        queries,
        kv,
    )


def choose(token_kv, positions, page_owner, queries, own_kv, selected, lengths):
    rows_here = queries.shape[0] // (2 * lax.axis_size("seq"))
    run = direct_body if rows_here == 8 else body
    return run(token_kv, positions, page_owner, queries, own_kv, selected, lengths)


def solution(mesh):
    in_specs = (
        P("role", ("groups", "seq"), None, None),
        P("role", ("groups", "seq")),
        P(("groups", "seq")),
        P("groups", None),
        P("groups", None, None),
        P("groups", None, None),
        P("groups"),
    )
    out_specs = (P(("groups", "role", "seq"), None), P(("groups", "role", "seq"), None))
    return jax.shard_map(choose, mesh=mesh, in_specs=in_specs, out_specs=out_specs, check_vma=False)
```
